128 devices in a mesh: side: 2 (over core), dev: 64 (over y, x, z).
Axes of the slice: x: 4, y: 4, z: 4, core: 2. Of those that a mesh axis runs over, the one named last changes fastest.
Arguments:
- out_gates: bfloat16 [2048, 2048], P('dev'), may hold values from -6 to 6
- queries: bfloat16 [2048, 2048], P('dev'), may hold values from -6 to 6
- keys_new: bfloat16 [2048, 256], P('dev'), may hold values from -6 to 6
- values_new: bfloat16 [2048, 256], P('dev'), may hold values from -6 to 6
- lengths: int32 [2048], P('dev'), may hold values from 1 to 128, as said below
- page_table: int32 [2048, 8], P('dev'), may hold values from 0 to 143, as said below
- cache_pool: bfloat16 [9216, 16, 512], P('dev'), may hold values from -1 to 1
- query_gain: float32 [256], replicated, may hold values from 0.25 to 1.75
- key_gain: float32 [256], replicated, may hold values from 0.25 to 1.75
- out_weight: bfloat16 [2048, 2048], replicated, may hold values from -0.125 to 0.125
- residual: bfloat16 [2048, 2048], P('dev'), may hold values from -0.625 to 0.625
- post_gain: float32 [2048], replicated, may hold values from 0.25 to 1.75
- experts: int32 [2048, 10], P('dev'), may hold values from 0 to 255, all different within a row; in each aligned block of 32 rows (0 to 31, 32 to 63, ...) at most 2 rows name the same one
- route_weights: float32 [2048, 10], P('dev'), may hold values from 0.05 to 1
- gate_weight: bfloat16 [256, 2048, 256], P('dev'), may hold values from -0.125 to 0.125
- up_weight: bfloat16 [256, 2048, 256], P('dev'), may hold values from -0.125 to 0.125
- down_weight: bfloat16 [256, 256, 2048], P('dev'), may hold values from -0.375 to 0.375
- shared_gate: bfloat16 [2048, 256], replicated, may hold values from -0.125 to 0.125
- shared_up: bfloat16 [2048, 256], replicated, may hold values from -0.125 to 0.125
- shared_down: bfloat16 [256, 2048], replicated, may hold values from -0.375 to 0.375
- shared_mix: bfloat16 [2048], replicated, may hold values from -0.125 to 0.125
Outputs:
- layer_out: bfloat16 [2048, 2048], P('dev', 'side')
The draws below stay inside these ranges and needn't reach their ends.
Inputs may be any that keep to these rules, and one draw needn't show every extreme that they name: Each row names 10 different experts; the rows of one device (aligned blocks of 32 rows) name one expert at most 2 times. A row's cache fills its first ceil(lengths / 16) page-table entries; in every device some row holds 128 tokens. `page_table`: indices are local to the row's device. The used entries of one device's rows name each of its 144 pages exactly once; unused entries name arbitrary pages.
All inputs are finite; a program needn't handle non-finite values.
Results may differ from the reference program's by a relative error of at most 0.024.
Values may be sent and summed in bfloat16 or wider, within the bound.
No kernel may reach another device: no remote copies, remote signals or barrier semaphores. Data moves between devices by JAX's collectives and lax.ppermute only.
A program may use at most 128 MiB of HBM per device.

```python
import math
import jax
import jax.numpy as jnp
import numpy as np
from jax import lax

D = 2048
HD = 256
HQ = 8
FE = 256
SFE = 256
TOPK = 10
PAGE = 16
MAXP = 8
ROWS_DEV = 32
EXPERTS = 256
CAP = 2
POOL_DEV = 144
ROWS = 2048
POOL = 9216
N_DEV = 64


def shared_pages(key):
    pairs = ROWS_DEV // 2
    first = jax.random.randint(jax.random.fold_in(key, 101), (N_DEV, pairs), 1, MAXP + 1)
    lead = jnp.arange(pairs, dtype=jnp.int32)[None, :] == 0
    first = jnp.where(lead, MAXP, first)
    count = jnp.stack([first, MAXP + 1 - first], axis=2).reshape(N_DEV, ROWS_DEV)
    offset = jax.random.randint(jax.random.fold_in(key, 102), (N_DEV, pairs, 2), 1, PAGE + 1)
    forced = lead[:, :, None] & (jnp.arange(2, dtype=jnp.int32)[None, None, :] == 0)
    offset = jnp.where(forced, PAGE, offset).reshape(N_DEV, ROWS_DEV)
    order_score = jax.random.randint(jax.random.fold_in(key, 103), (N_DEV, ROWS_DEV), 0, 1 << 20) * ROWS_DEV + jnp.arange(ROWS_DEV, dtype=jnp.int32)[None, :]
    order = jnp.argsort(order_score, axis=1)
    count = jnp.take_along_axis(count, order, axis=1)
    offset = jnp.take_along_axis(offset, order, axis=1)
    lengths = (count - 1) * PAGE + offset
    start = jnp.cumsum(count, axis=1) - count
    pool_score = jax.random.randint(jax.random.fold_in(key, 104), (N_DEV, POOL_DEV), 0, 1 << 20) * POOL_DEV + jnp.arange(POOL_DEV, dtype=jnp.int32)[None, :]
    pool_order = jnp.argsort(pool_score, axis=1).astype(jnp.int32)
    entry = jnp.arange(MAXP, dtype=jnp.int32)[None, None, :]
    position = jnp.minimum(start[:, :, None] + entry, POOL_DEV - 1).reshape(N_DEV, ROWS_DEV * MAXP)
    named = jnp.take_along_axis(pool_order, position, axis=1).reshape(N_DEV, ROWS_DEV, MAXP)
    spare = jax.random.randint(jax.random.fold_in(key, 105), (N_DEV, ROWS_DEV, MAXP), 0, POOL_DEV)
    table = jnp.where(entry < count[:, :, None], named, spare)
    return (lengths.reshape(ROWS_DEV * N_DEV).astype(jnp.int32), table.reshape(ROWS_DEV * N_DEV, MAXP).astype(jnp.int32))


def draw_lengths(key, part):
    both = shared_pages(key)
    return both[0]


def draw_page_table(key, part):
    both = shared_pages(key)
    return both[1]


def shard_levels(stream_key, shape, shards, least, largest):
    level = 1.0
    for axis_at, blocks in shards:
        draws = jax.random.uniform(jax.random.fold_in(jax.random.fold_in(stream_key, 6), axis_at), (blocks,), jnp.float32, least / len(shards), largest / len(shards))
        level = level * jnp.repeat(jnp.exp(draws), shape[axis_at] // blocks).reshape((-1,) + (1,) * (len(shape) - 1 - axis_at))
    return level


def routed_block(rng, own, number, rows, number_of, top, limit, skew):
    ranking = jax.random.permutation(rng, number_of)
    packed, usual = shares(number_of, rows * top, limit, skew, True), shares(number_of, rows * top, limit, skew, False)
    places = jnp.arange(number_of)

    def named(sizes, rotation):
        used = int((sizes > 0).sum())
        fixed = max(1, used // 4)
        passed = fixed + (places - fixed + rotation * (used - fixed)) % max(1, number_of - fixed)
        return jnp.zeros((number_of,), jnp.int32).at[ranking[jnp.where(places < fixed, places, passed)]].set(jnp.asarray(sizes, jnp.int32))

    sizes = jnp.where(number % 4 == 0, named(packed, number // 4), named(usual, number - number // 4 - 1))
    mixed = jax.random.permutation(jax.random.fold_in(own, 3), number_of)
    source_of, taker = mixed[0:number_of // 2 * 2:2], mixed[1:number_of // 2 * 2:2]
    room = jnp.minimum(sizes[source_of] - 1, limit - sizes[taker]) // 2
    room = jnp.where((source_of == ranking[0]) | (taker == ranking[0]) | (sizes[taker] == 0), 0, jnp.maximum(room, 0))
    passed = jax.random.randint(jax.random.fold_in(own, 4), (number_of // 2,), 0, 1 << 20) % (room + 1)
    sizes = sizes.at[source_of].add(-passed).at[taker].add(passed)
    members = jnp.searchsorted(jnp.cumsum(sizes), jnp.arange(rows * top), side="right").astype(jnp.int32)
    grid = members.reshape(top, rows).T
    grid = grid[jax.random.permutation(jax.random.fold_in(own, 1), rows)]
    rotation = jax.random.randint(jax.random.fold_in(own, 2), (rows, 1), 0, top)
    return jnp.take_along_axis(grid, (jnp.arange(top)[None, :] + rotation) % top, axis=1)


def shares(count, total, most, skew, full):
    weights = [(1 << 20) // math.isqrt(standing ** skew) + 1 for standing in range(1, count + 1)]
    largest = most if full else min(most, max(-(-total // count), total * weights[0] // sum(weights)))
    least = 1 if total - largest >= count - 1 else 0
    holding, spare = [largest] + [least] * (count - 1), total - largest - least * (count - 1)
    while spare > 0:
        movable = [i for i in range(1, count) if holding[i] < largest] or [i for i in range(1, count) if holding[i] < most]
        pool, budget = sum([weights[i] for i in movable]), spare
        for i in movable:
            addition = min(most - holding[i], max(1, budget * weights[i] // pool), spare)
            holding[i] = holding[i] + addition
            spare = spare - addition
    return np.array(holding)


def gaussian(own_key, extent, spread, reach, split=(), held_as=jnp.bfloat16):
    level = shard_levels(own_key, extent, split, -0.22, 0.18) if split else 1.0
    result = jax.random.normal(own_key, extent, jnp.float32) * spread * level
    return jnp.minimum(jnp.maximum(result, -reach), reach).astype(held_as)


def setup_inputs(seed: int = 0) -> dict:
    arg_keys = jax.random.split(jax.random.key(seed), 22)
    out_gates = gaussian(arg_keys[0], (ROWS, HQ * HD), 1.0, 6.0, ((0, 64),))
    queries = gaussian(arg_keys[1], (ROWS, HQ * HD), 1.0, 6.0, ((0, 64),))
    keys_new = gaussian(arg_keys[2], (ROWS, HD), 1.0, 6.0, ((0, 64),))
    values_new = gaussian(arg_keys[3], (ROWS, HD), 1.0, 6.0, ((0, 64),))
    lengths = draw_lengths(jax.random.fold_in(arg_keys[21], 71), 0)
    page_table = draw_page_table(jax.random.fold_in(arg_keys[21], 71), 0)
    cache_pool = jnp.clip(jax.random.uniform(arg_keys[6], (POOL, PAGE, 2 * HD), jnp.float32, -1.0, 1.0) * shard_levels(arg_keys[6], (POOL, PAGE, 2 * HD), ((0, 64),), -0.4, 0.0), -1.0, 1.0).astype(jnp.bfloat16)
    query_gain = jnp.clip(1.0 + 0.15 * jax.random.normal(arg_keys[7], (HD,), jnp.float32), 0.25, 1.75)
    key_gain = jnp.clip(1.0 + 0.15 * jax.random.normal(arg_keys[8], (HD,), jnp.float32), 0.25, 1.75)
    out_weight = gaussian(arg_keys[9], (HQ * HD, D), (HQ * HD) ** -0.5, 0.125)
    residual = gaussian(arg_keys[10], (ROWS, D), 0.1, 0.625, ((0, 64),))
    post_gain = jnp.clip(1.0 + 0.15 * jax.random.normal(arg_keys[11], (D,), jnp.float32), 0.25, 1.75)
    experts_keys = jax.random.split(jax.random.fold_in(arg_keys[12], 1), ROWS // ROWS_DEV)
    experts_turns = jax.random.permutation(jax.random.fold_in(arg_keys[12], 3), ROWS // ROWS_DEV)
    experts = jax.vmap(lambda own, number: routed_block(jax.random.fold_in(arg_keys[12], 2), own, number, ROWS_DEV, EXPERTS, TOPK, CAP, 2))(experts_keys, experts_turns).reshape((ROWS, TOPK))
    route_weights = jnp.clip(jnp.exp(math.log(1.0) - 2.9957323 * jax.random.uniform(arg_keys[13], (ROWS, TOPK), jnp.float32) ** shard_levels(arg_keys[13], (ROWS, TOPK), ((0, 64),), -0.2, 0.2)), 0.05, 1.0)
    gate_weight = gaussian(arg_keys[14], (EXPERTS, D, FE), D ** -0.5, 0.125, ((0, 64),))
    up_weight = gaussian(arg_keys[15], (EXPERTS, D, FE), D ** -0.5, 0.125, ((0, 64),))
    down_weight = gaussian(arg_keys[16], (EXPERTS, FE, D), FE ** -0.5, 0.375, ((0, 64),))
    shared_gate = gaussian(arg_keys[17], (D, SFE), D ** -0.5, 0.125)
    shared_up = gaussian(arg_keys[18], (D, SFE), D ** -0.5, 0.125)
    shared_down = gaussian(arg_keys[19], (SFE, D), SFE ** -0.5, 0.375)
    shared_mix = gaussian(arg_keys[20], (D,), D ** -0.5, 0.125)
    return dict(out_gates=out_gates, queries=queries, keys_new=keys_new, values_new=values_new, lengths=lengths, page_table=page_table, cache_pool=cache_pool, query_gain=query_gain, key_gain=key_gain, out_weight=out_weight, residual=residual, post_gain=post_gain, experts=experts, route_weights=route_weights, gate_weight=gate_weight, up_weight=up_weight, down_weight=down_weight, shared_gate=shared_gate, shared_up=shared_up, shared_down=shared_down, shared_mix=shared_mix)


eps = 1e-06

def rms_scale(values, gain):
    wide = values.astype(jnp.float32)
    return wide * lax.rsqrt(lax.optimization_barrier(jnp.mean(wide * wide, axis=-1, keepdims=True)) + eps) * gain.astype(jnp.float32)

def reference(out_gates, queries, keys_new, values_new, lengths, page_table, cache_pool, query_gain, key_gain, out_weight, residual, post_gain, experts, route_weights, gate_weight, up_weight, down_weight, shared_gate, shared_up, shared_down, shared_mix):
    scale = HD ** (-0.5)

    def one_device(block):
        gates_in, queries_in, keys_in, values_in, lengths_in, table_in, pool_in = block
        rows = queries_in.shape[0]
        query_normed = rms_scale(queries_in.reshape(rows, HQ, HD), query_gain).astype(jnp.bfloat16)
        key_normed = rms_scale(keys_in, key_gain).astype(jnp.bfloat16)
        pages = pool_in[table_in].reshape(rows, MAXP * PAGE, 2 * HD)
        cached_keys = pages[:, :, :HD].astype(jnp.float32)
        cached_values = pages[:, :, HD:].astype(jnp.float32)
        query_wide = query_normed.astype(jnp.float32)
        scores = jnp.einsum('rhd,rtd->rht', query_wide, cached_keys) * scale
        own = jnp.einsum('rhd,rd->rh', query_wide, key_normed.astype(jnp.float32)) * scale
        valid = jnp.arange(MAXP * PAGE, dtype=jnp.int32)[None, None, :] < lengths_in[:, None, None]
        weights = jnp.where(valid, jnp.exp(scores), 0.0)
        own_weight = jnp.exp(own)
        total = lax.optimization_barrier(jnp.sum(weights, axis=2)) + own_weight
        probs = (weights / total[:, :, None]).astype(jnp.bfloat16)
        own_prob = (own_weight / total).astype(jnp.bfloat16)
        mixed = jnp.einsum('rht,rtd->rhd', probs.astype(jnp.float32), cached_values)
        mixed = mixed + own_prob.astype(jnp.float32)[:, :, None] * values_in.astype(jnp.float32)[:, None, :]
        gated = mixed * jax.nn.sigmoid(gates_in.reshape(rows, HQ, HD).astype(jnp.float32))
        return gated.reshape(rows, HQ * HD).astype(jnp.bfloat16)
    blocks = (out_gates.reshape(N_DEV, ROWS_DEV, HQ * HD), queries.reshape(N_DEV, ROWS_DEV, HQ * HD), keys_new.reshape(N_DEV, ROWS_DEV, HD), values_new.reshape(N_DEV, ROWS_DEV, HD), lengths.reshape(N_DEV, ROWS_DEV), page_table.reshape(N_DEV, ROWS_DEV, MAXP), cache_pool.reshape(N_DEV, POOL_DEV, PAGE, 2 * HD))
    attended = lax.map(one_device, blocks).reshape(ROWS, HQ * HD)
    projected = jnp.dot(attended, out_weight, preferred_element_type=jnp.float32)
    hidden = (residual.astype(jnp.float32) + projected).astype(jnp.bfloat16)
    normed = rms_scale(hidden, post_gain).astype(jnp.bfloat16)
    slots_each = N_DEV * CAP
    flat = experts.reshape(-1).astype(jnp.int32)
    onehot = (flat[:, None] == jnp.arange(EXPERTS, dtype=jnp.int32)[None, :]).astype(jnp.int32)
    rank = lax.optimization_barrier(jnp.sum((jnp.cumsum(onehot, axis=0) - 1) * onehot, axis=1)).astype(jnp.int32)
    slot = (flat * slots_each + rank).astype(jnp.int32)
    source = jnp.repeat(jnp.arange(ROWS, dtype=jnp.int32), TOPK)
    buffer = jnp.zeros((EXPERTS * slots_each, D), jnp.bfloat16).at[slot].set(normed[source])

    def run_expert(item):
        rows_in, gate_in, up_in, down_in = item
        gate_val = jnp.dot(rows_in, gate_in, preferred_element_type=jnp.float32)
        up_val = jnp.dot(rows_in, up_in, preferred_element_type=jnp.float32)
        inner = (jax.nn.silu(gate_val) * up_val).astype(jnp.bfloat16)
        return jnp.dot(inner, down_in, preferred_element_type=jnp.float32).astype(jnp.bfloat16)
    results = lax.map(run_expert, (buffer.reshape(EXPERTS, slots_each, D), gate_weight, up_weight, down_weight))
    picked = results.reshape(EXPERTS * slots_each, D)[slot].reshape(ROWS, TOPK, D)
    share = route_weights / lax.optimization_barrier(jnp.sum(route_weights, axis=1, keepdims=True))
    routed = jnp.einsum('rk,rkd->rd', share, picked.astype(jnp.float32))
    shared_gate_val = jnp.dot(normed, shared_gate, preferred_element_type=jnp.float32)
    shared_up_val = jnp.dot(normed, shared_up, preferred_element_type=jnp.float32)
    shared_inner = (jax.nn.silu(shared_gate_val) * shared_up_val).astype(jnp.bfloat16)
    shared_out = jnp.dot(shared_inner, shared_down, preferred_element_type=jnp.float32)
    shared_weight = jax.nn.sigmoid(jnp.dot(normed, shared_mix, preferred_element_type=jnp.float32))
    total_out = hidden.astype(jnp.float32) + routed + shared_weight[:, None] * shared_out
    return total_out.astype(jnp.bfloat16)
```

```python
import functools
import jax
import jax.numpy as jnp
from jax import lax
from jax.experimental import pallas as pl
from jax.experimental.pallas import tpu as pltpu
from jax.sharding import PartitionSpec as P

eps = 1e-06
f32 = jnp.float32
bf16 = jnp.bfloat16
i32 = jnp.int32
MIB = 1 << 20


def dot(left, right):
    return jnp.dot(left, right, preferred_element_type=f32)


def iota(shape, axis):
    return lax.broadcasted_iota(i32, shape, axis)


def rms_scale(wide, gain):
    return wide * lax.rsqrt(jnp.mean(wide * wide, axis=-1, keepdims=True) + eps) * gain


def group_order(groups, members, to_groups):
    size = groups * members
    by_group = iota((size, size), 0 if to_groups else 1)
    by_member = iota((size, size), 1 if to_groups else 0)
    wanted = (by_group % members) * groups + by_group // members
    return (wanted == by_member).astype(f32).astype(bf16)


def expert_hits(experts_ref, slot_expert):
    rows, topk = experts_ref.shape
    hits = jnp.zeros(slot_expert.shape, f32)
    for k in range(topk):
        hits = jnp.where(experts_ref[:, k : k + 1] == slot_expert, 1.0, hits)
    earlier = (iota((rows, rows), 1) < iota((rows, rows), 0)).astype(f32).astype(bf16)
    rank = dot(earlier, hits.astype(bf16))
    return hits, rank


def front_kernel(
    lengths_ref,
    table_ref,
    experts_ref,
    gates_ref,
    queries_ref,
    keys_ref,
    values_ref,
    query_gain_ref,
    key_gain_ref,
    post_gain_ref,
    residual_ref,
    pool_hbm,
    weight_hbm,
    packed_ref,
    hidden_ref,
    normed_ref,
    pool,
    weight,
    query,
    prob,
    attended,
    pool_sem,
    weight_sem,
    *,
    page,
    local,
):
    rows, width = queries_ref.shape
    head = keys_ref.shape[1]
    heads = width // head
    tokens = pool.shape[0]
    context = 256
    chunks = tokens // context
    side = lax.axis_index("side")

    pool_copies = []
    third = tokens // pool_sem.shape[0]
    for i in range(pool_sem.shape[0]):
        part = pl.ds(i * third, third)
        pool_copies.append(
            pltpu.make_async_copy(pool_hbm.at[part], pool.at[part], pool_sem.at[i])
        )
    weight_copies = []
    quarter = width // weight_sem.shape[0]
    for i in range(weight_sem.shape[0]):
        part = pl.ds(i * quarter, quarter)
        weight_copies.append(
            pltpu.make_async_copy(weight_hbm.at[part], weight.at[part], weight_sem.at[i])
        )
    for copy in pool_copies + weight_copies:
        copy.start()

    scale = head ** (-0.5)
    key_normed = rms_scale(keys_ref[...].astype(f32), key_gain_ref[...]).astype(bf16).astype(f32)
    own = []
    for h in range(heads):
        part = queries_ref[:, h * head : (h + 1) * head].astype(f32)
        normed = rms_scale(part, query_gain_ref[...]).astype(bf16)
        query[h * rows : (h + 1) * rows, :] = normed
        own.append(jnp.sum(normed.astype(f32) * key_normed, axis=-1, keepdims=True))
    own_weight = jnp.exp(jnp.concatenate(own, axis=0) * scale)

    same = iota((rows, rows), 0) == iota((rows, rows), 1)
    lengths = jnp.sum(
        jnp.where(same, jnp.broadcast_to(lengths_ref[...], (rows, rows)), 0), axis=1, keepdims=True
    )
    total = jnp.zeros((heads * rows, context), f32)
    for c in range(chunks):
        if (c * context) % third == 0:
            pool_copies[c * context // third].wait()
        at = pl.ds(c * context, context)
        token = iota((rows, context), 1) + c * context
        token_page = token // page
        token_in = token % page
        valid = jnp.zeros((rows, context), f32)
        for entry in range(table_ref.shape[1]):
            hit = (table_ref[:, entry : entry + 1] == token_page) & (
                token_in + entry * page < lengths
            )
            valid = jnp.where(hit, 1.0, valid)
        scores = lax.dot_general(
            query[...],
            pool[at, :head],
            (((1,), (1,)), ((), ())),
            preferred_element_type=f32,
        )
        weights = jnp.exp(scores * scale)
        weights = (weights.reshape(heads, rows, context) * valid[None]).reshape(
            heads * rows, context
        )
        total = total + weights
        prob[:, at] = weights.astype(bf16)
    mixed = dot(prob[...], pool[:, head:])
    inverse = 1.0 / (jnp.sum(total, axis=1, keepdims=True) + own_weight)
    new_values = values_ref[...].astype(f32)
    for h in range(heads):
        part = slice(h * rows, (h + 1) * rows)
        value = (mixed[part] + own_weight[part] * new_values) * inverse[part]
        gate = jax.nn.sigmoid(gates_ref[:, h * head : (h + 1) * head].astype(f32))
        attended[:, h * head : (h + 1) * head] = (value * gate).astype(bf16)

    projected = residual_ref[...].astype(f32)
    for i, copy in enumerate(weight_copies):
        copy.wait()
        at = slice(i * quarter, (i + 1) * quarter)
        projected = projected + dot(attended[:, at], weight[at, :])
    hidden = projected.astype(bf16)
    hidden_ref[...] = hidden
    normed = rms_scale(hidden.astype(f32), post_gain_ref[...]).astype(bf16)
    normed_ref[...] = normed

    slots, columns = packed_ref.shape
    parts = width // columns
    mine = local // 2
    slot = iota((rows, slots), 1)
    per = parts * mine
    destination = slot // per
    n_dev = slots // per // 2
    expert = (destination % n_dev) * local + (destination // n_dev) * mine + slot % mine
    hits, rank = expert_hits(experts_ref, expert)
    chosen = jnp.where(rank == side.astype(f32), hits, 0.0)
    slot_part = slot % per // mine
    spread = jnp.concatenate(
        [jnp.where(slot_part == p, chosen, 0.0) for p in range(parts)], axis=0
    )
    stacked = jnp.concatenate(
        [normed[:, p * columns : (p + 1) * columns] for p in range(parts)], axis=0
    )
    packed_ref[...] = dot(spread.T.astype(bf16), stacked).astype(bf16)


def expert_kernel(
    normed_ref,
    hidden_ref,
    mix_ref,
    received_hbm,
    gate_hbm,
    up_hbm,
    down_hbm,
    shared_gate_hbm,
    shared_up_hbm,
    shared_down_hbm,
    sent_ref,
    base_ref,
    received,
    gate,
    up,
    down,
    shared_gate,
    shared_up,
    shared_down,
    taken,
    result,
    sem,
):
    mine, width, inner_width = gate.shape
    slots, columns = received.shape
    parts = width // columns
    rows = slots // (parts * mine)
    half = width // 2
    side = lax.axis_index("side")
    experts_at = pl.ds(side * mine, mine)
    columns_at = pl.ds(pl.multiple_of(side * half, half), half)
    copies = [
        pltpu.make_async_copy(source, target, sem.at[i])
        for i, (source, target) in enumerate(
            (
                (received_hbm, received),
                (shared_gate_hbm, shared_gate),
                (shared_up_hbm, shared_up),
                (gate_hbm.at[experts_at], gate),
                (up_hbm.at[experts_at], up),
                (shared_down_hbm.at[:, columns_at], shared_down),
                (down_hbm.at[experts_at], down),
            )
        )
    ]
    for copy in copies:
        copy.start()
    groups = parts * mine
    block = 32
    inward = group_order(groups, block, True)
    outward = group_order(groups, block, False)

    copies[0].wait()
    for b in range(rows // block):
        ordered = dot(inward, received[b * groups * block : (b + 1) * groups * block, :]).astype(
            bf16
        )
        for p in range(parts):
            for j in range(mine):
                at = (p * mine + j) * block
                taken[j, b * block : (b + 1) * block, p * columns : (p + 1) * columns] = ordered[
                    at : at + block
                ]

    copies[1].wait()
    copies[2].wait()
    normed = normed_ref[...]
    shared_inner = (
        jax.nn.silu(dot(normed, shared_gate[...])) * dot(normed, shared_up[...])
    ).astype(bf16)
    mix = jax.nn.sigmoid(
        jnp.sum(normed.astype(f32) * mix_ref[...].astype(f32), axis=-1, keepdims=True)
    )
    copies[3].wait()
    copies[4].wait()
    inner = [
        (jax.nn.silu(dot(taken[j], gate[j])) * dot(taken[j], up[j])).astype(bf16)
        for j in range(mine)
    ]
    copies[5].wait()
    base_ref[...] = hidden_ref[:, columns_at].astype(f32) + mix * dot(
        shared_inner, shared_down[...]
    )
    copies[6].wait()
    for j in range(mine):
        result[j] = dot(inner[j], down[j]).astype(bf16)

    n_dev = rows // 2
    for t in range(2):
        for b in range(n_dev // block):
            gathered = jnp.concatenate(
                [
                    result[
                        j,
                        s * n_dev + b * block : s * n_dev + (b + 1) * block,
                        t * half + p * columns : t * half + (p + 1) * columns,
                    ]
                    for p in range(half // columns)
                    for s in range(2)
                    for j in range(mine)
                ],
                axis=0,
            )
            at = (t * n_dev + b * block) * groups
            sent_ref[at : at + groups * block, :] = dot(outward, gathered).astype(bf16)


def combine_kernel(
    experts_ref, weights_ref, base_ref, returned_hbm, out_ref, returned, sem, *, local
):
    copy = pltpu.make_async_copy(returned_hbm, returned, sem.at[0])
    copy.start()
    rows, topk = experts_ref.shape
    slots, columns = returned.shape
    parts = out_ref.shape[1] // columns
    mine = local // 2
    per = parts * 2 * mine
    slot = iota((rows, slots), 1)
    source = slot // per
    n_dev = slots // per // 2
    expert = (source % n_dev) * local + (source // n_dev) * mine + slot % mine
    weights = weights_ref[...]
    share = weights / jnp.sum(weights, axis=1, keepdims=True)
    spread = jnp.zeros((rows, slots), f32)
    for k in range(topk):
        spread = jnp.where(experts_ref[:, k : k + 1] == expert, share[:, k : k + 1], spread)
    hits, rank = expert_hits(experts_ref, expert)
    sender = slot % (2 * mine) // mine
    spread = jnp.where(rank == sender.astype(f32), spread, 0.0)
    slot_part = slot % per // (2 * mine)
    pieces = []
    for p in range(parts):
        piece = jnp.where(slot_part == p, spread, 0.0)
        high = piece.astype(bf16)
        pieces.append(high)
        pieces.append((piece - high.astype(f32)).astype(bf16))
    stacked = jnp.concatenate(pieces, axis=0)
    copy.wait()
    routed = dot(stacked, returned[...])
    for p in range(parts):
        at = 2 * p * rows
        value = routed[at : at + rows] + routed[at + rows : at + 2 * rows]
        out_ref[:, p * columns : (p + 1) * columns] = (
            base_ref[:, p * columns : (p + 1) * columns] + value
        ).astype(bf16)


VMEM = pl.BlockSpec(memory_space=pltpu.VMEM)
HBM = pl.BlockSpec(memory_space=pl.ANY)


def exchange(value):
    return lax.all_to_all(value, ("side", "dev"), split_axis=0, concat_axis=0, tiled=True)


def on_device(
    out_gates,
    queries,
    keys_new,
    values_new,
    lengths,
    page_table,
    cache_pool,
    query_gain,
    key_gain,
    out_weight,
    residual,
    post_gain,
    experts,
    route_weights,
    gate_weight,
    up_weight,
    down_weight,
    shared_gate,
    shared_up,
    shared_down,
    shared_mix,
):
    n_dev = lax.axis_size("dev")
    local, width, inner_width = gate_weight.shape
    rows = queries.shape[0]
    head = keys_new.shape[1]
    heads = width // head
    pages, page, both = cache_pool.shape
    tokens = pages * page
    mine = local // 2
    columns = width * mine // 8
    slots = 2 * n_dev * 8
    packed, hidden, normed = pl.pallas_call(
        functools.partial(front_kernel, page=page, local=local),
        out_shape=(
            jax.ShapeDtypeStruct((slots, columns), bf16),
            jax.ShapeDtypeStruct((rows, width), bf16),
            jax.ShapeDtypeStruct((rows, width), bf16),
        ),
        in_specs=[VMEM] * 11 + [HBM] * 2,
        out_specs=(VMEM, VMEM, VMEM),
        scratch_shapes=[
            pltpu.VMEM((tokens, both), bf16),
            pltpu.VMEM((width, width), bf16),
            pltpu.VMEM((heads * rows, head), bf16),
            pltpu.VMEM((heads * rows, tokens), bf16),
            pltpu.VMEM((rows, width), bf16),
            pltpu.SemaphoreType.DMA((3,)),
            pltpu.SemaphoreType.DMA((4,)),
        ],
        compiler_params=pltpu.CompilerParams(vmem_limit_bytes=40 * MIB),
    )(
        lengths[None, :],
        page_table,
        experts,
        out_gates,
        queries,
        keys_new,
        values_new,
        query_gain[None, :],
        key_gain[None, :],
        post_gain[None, :],
        residual,
        cache_pool.reshape(tokens, both),
        out_weight,
    )
    received = exchange(packed)
    half = width // 2
    sent, base = pl.pallas_call(
        expert_kernel,
        out_shape=(
            jax.ShapeDtypeStruct((slots, columns), bf16),
            jax.ShapeDtypeStruct((rows, half), f32),
        ),
        in_specs=[VMEM] * 3 + [HBM] * 7,
        out_specs=(VMEM, VMEM),
        scratch_shapes=[
            pltpu.VMEM((slots, columns), bf16),
            pltpu.VMEM((mine, width, inner_width), bf16),
            pltpu.VMEM((mine, width, inner_width), bf16),
            pltpu.VMEM((mine, inner_width, width), bf16),
            pltpu.VMEM(shared_gate.shape, bf16),
            pltpu.VMEM(shared_up.shape, bf16),
            pltpu.VMEM((shared_down.shape[0], half), bf16),
            pltpu.VMEM((mine, 2 * n_dev, width), bf16),
            pltpu.VMEM((mine, 2 * n_dev, width), bf16),
            pltpu.SemaphoreType.DMA((7,)),
        ],
        compiler_params=pltpu.CompilerParams(vmem_limit_bytes=40 * MIB),
    )(
        normed,
        hidden,
        shared_mix[None, :],
        received,
        gate_weight,
        up_weight,
        down_weight,
        shared_gate,
        shared_up,
        shared_down,
    )
    returned = exchange(sent)
    return pl.pallas_call(
        functools.partial(combine_kernel, local=local),
        out_shape=jax.ShapeDtypeStruct((rows, half), bf16),
        in_specs=[VMEM] * 3 + [HBM],
        out_specs=VMEM,
        scratch_shapes=[
            pltpu.VMEM((slots, columns), bf16),
            pltpu.SemaphoreType.DMA((1,)),
        ],
        compiler_params=pltpu.CompilerParams(vmem_limit_bytes=40 * MIB),
    )(experts, route_weights, base, returned)


def solution(mesh):
    placed = (
        P("dev", None),
        P("dev", None),
        P("dev", None),
        P("dev", None),
        P("dev"),
        P("dev", None),
        P("dev", None, None),
        P(),
        P(),
        P(),
        P("dev", None),
        P(),
        P("dev", None),
        P("dev", None),
        P("dev", None, None),
        P("dev", None, None),
        P("dev", None, None),
        P(),
        P(),
        P(),
        P(),
    )
    return jax.shard_map(
        on_device, mesh=mesh, in_specs=placed, out_specs=P("dev", "side"), check_vma=False
    )
```

```python
import functools
import jax
import jax.numpy as jnp
from jax import lax
from jax.experimental import pallas as pl
from jax.experimental.pallas import tpu as pltpu
from jax.sharding import PartitionSpec as P

eps = 1e-06
f32 = jnp.float32
bf16 = jnp.bfloat16
i32 = jnp.int32
MIB = 1 << 20


def dot(left, right):
    return jnp.dot(left, right, preferred_element_type=f32)


def iota(shape, axis):
    return lax.broadcasted_iota(i32, shape, axis)


def rms_scale(wide, gain):
    return wide * lax.rsqrt(jnp.mean(wide * wide, axis=-1, keepdims=True) + eps) * gain


def group_order(groups, members, to_groups):
    size = groups * members
    by_group = iota((size, size), 0 if to_groups else 1)
    by_member = iota((size, size), 1 if to_groups else 0)
    wanted = (by_group % members) * groups + by_group // members
    return (wanted == by_member).astype(f32).astype(bf16)


def expert_hits(experts, slot_expert):
    rows, topk = experts.shape
    hits = jnp.zeros(slot_expert.shape, f32)
    for k in range(topk):
        hits = jnp.where(experts[:, k : k + 1] == slot_expert, 1.0, hits)
    earlier = (iota((rows, rows), 1) < iota((rows, rows), 0)).astype(f32).astype(bf16)
    rank = dot(earlier, hits.astype(bf16))
    return hits, rank


def start_all(pairs, sem):
    copies = [
        pltpu.make_async_copy(source, target, sem.at[i]) for i, (source, target) in enumerate(pairs)
    ]
    for copy in copies:
        copy.start()
    return copies


def pieces_of(source, target, count):
    size = source.shape[0] // count
    return [
        (source.at[pl.ds(i * size, size)], target.at[pl.ds(i * size, size)]) for i in range(count)
    ]


def front_kernel(*refs, page, local):
    sources, refs = refs[:13], refs[13:]
    packed_ref, hidden_ref, normed_ref = refs[:3]
    targets, refs = refs[3:16], refs[16:]
    query, prob, attended, sem = refs
    pool_hbm, weight_hbm = sources[-2:]
    (
        lengths_ref,
        table_in,
        experts_in,
        queries_ref,
        query_gain_ref,
        keys_ref,
        key_gain_ref,
        values_ref,
        gates_ref,
        residual_ref,
        post_gain_ref,
        pool,
        weight,
    ) = targets
    rows, width = queries_ref.shape
    head = keys_ref.shape[1]
    heads = width // head
    tokens = pool.shape[0]
    context = 256
    chunks = tokens // context
    pool_parts = 3
    weight_parts = 4
    third = tokens // pool_parts
    quarter = width // weight_parts
    side = lax.axis_index("side")
    pairs = list(zip(sources, targets))
    copies = start_all(
        pairs[:7]
        + pieces_of(pool_hbm, pool, pool_parts)
        + pairs[7:11]
        + pieces_of(weight_hbm, weight, weight_parts),
        sem,
    )
    pool_copies = copies[7 : 7 + pool_parts]
    late_copies = copies[7 + pool_parts : 11 + pool_parts]
    weight_copies = copies[11 + pool_parts :]
    for copy in copies[:7]:
        copy.wait()
    table = table_in[...].T

    scale = head ** (-0.5)
    key_normed = rms_scale(keys_ref[...].astype(f32), key_gain_ref[...]).astype(bf16).astype(f32)
    own = []
    for h in range(heads):
        part = queries_ref[:, h * head : (h + 1) * head].astype(f32)
        normed = rms_scale(part, query_gain_ref[...]).astype(bf16)
        query[h * rows : (h + 1) * rows, :] = normed
        own.append(jnp.sum(normed.astype(f32) * key_normed, axis=-1, keepdims=True))
    own_weight = jnp.exp(jnp.concatenate(own, axis=0) * scale)

    same = iota((rows, rows), 0) == iota((rows, rows), 1)
    lengths = jnp.sum(
        jnp.where(same, jnp.broadcast_to(lengths_ref[...], (rows, rows)), 0), axis=1, keepdims=True
    )
    total = jnp.zeros((heads * rows, context), f32)
    for c in range(chunks):
        if (c * context) % third == 0:
            pool_copies[c * context // third].wait()
        at = pl.ds(c * context, context)
        token = iota((rows, context), 1) + c * context
        token_page = token // page
        token_in = token % page
        valid = jnp.zeros((rows, context), f32)
        for entry in range(table.shape[1]):
            hit = (table[:, entry : entry + 1] == token_page) & (
                token_in + entry * page < lengths
            )
            valid = jnp.where(hit, 1.0, valid)
        scores = lax.dot_general(
            query[...],
            pool[at, :head],
            (((1,), (1,)), ((), ())),
            preferred_element_type=f32,
        )
        weights = jnp.exp(scores * scale)
        weights = (weights.reshape(heads, rows, context) * valid[None]).reshape(
            heads * rows, context
        )
        total = total + weights
        prob[:, at] = weights.astype(bf16)
    mixed = dot(prob[...], pool[:, head:])
    for copy in late_copies:
        copy.wait()
    inverse = 1.0 / (jnp.sum(total, axis=1, keepdims=True) + own_weight)
    new_values = values_ref[...].astype(f32)
    for h in range(heads):
        part = slice(h * rows, (h + 1) * rows)
        value = (mixed[part] + own_weight[part] * new_values) * inverse[part]
        gate = jax.nn.sigmoid(gates_ref[:, h * head : (h + 1) * head].astype(f32))
        attended[:, h * head : (h + 1) * head] = (value * gate).astype(bf16)

    projected = residual_ref[...].astype(f32)
    for i, copy in enumerate(weight_copies):
        copy.wait()
        at = slice(i * quarter, (i + 1) * quarter)
        projected = projected + dot(attended[:, at], weight[at, :])
    hidden = projected.astype(bf16)
    hidden_ref[...] = hidden
    normed = rms_scale(hidden.astype(f32), post_gain_ref[...]).astype(bf16)
    normed_ref[...] = normed

    slots, columns = packed_ref.shape
    parts = width // columns
    mine = local // 2
    slot = iota((rows, slots), 1)
    per = parts * mine
    destination = slot // per
    n_dev = slots // per // 2
    expert = (destination % n_dev) * local + (destination // n_dev) * mine + slot % mine
    hits, rank = expert_hits(experts_in[...].T, expert)
    chosen = jnp.where(rank == side.astype(f32), hits, 0.0)
    slot_part = slot % per // mine
    spread = jnp.concatenate(
        [jnp.where(slot_part == p, chosen, 0.0) for p in range(parts)], axis=0
    )
    stacked = jnp.concatenate(
        [normed[:, p * columns : (p + 1) * columns] for p in range(parts)], axis=0
    )
    packed_ref[...] = dot(spread.T.astype(bf16), stacked).astype(bf16)


def middle_kernel(
    normed_ref,
    hidden_ref,
    experts_hbm,
    weights_hbm,
    mix_hbm,
    shared_gate_hbm,
    shared_up_hbm,
    shared_down_hbm,
    gate_hbm,
    up_hbm,
    down_hbm,
    base_ref,
    spread_ref,
    gate_ref,
    up_ref,
    down_ref,
    experts_in,
    weights_in,
    mix,
    shared_gate,
    shared_up,
    shared_down,
    sem,
    *,
    n_dev,
):
    rows, width = normed_ref.shape
    half = width // 2
    local = gate_hbm.shape[0]
    mine = local // 2
    side = lax.axis_index("side")
    experts_at = pl.ds(side * mine, mine)
    columns_at = pl.ds(pl.multiple_of(side * half, half), half)
    copies = start_all(
        [
            (experts_hbm, experts_in),
            (weights_hbm, weights_in),
            (mix_hbm, mix),
            (shared_gate_hbm, shared_gate),
            (shared_up_hbm, shared_up),
            (shared_down_hbm.at[:, columns_at], shared_down),
            (gate_hbm.at[experts_at], gate_ref),
            (up_hbm.at[experts_at], up_ref),
            (down_hbm.at[experts_at], down_ref),
        ],
        sem,
    )
    for copy in copies[:2]:
        copy.wait()
    experts = experts_in[...].T
    weights = weights_in[...].T
    slots = spread_ref.shape[1]
    per = slots // (2 * n_dev)
    parts = per // local
    slot = iota((rows, slots), 1)
    source = slot // per
    expert = (source % n_dev) * local + (source // n_dev) * mine + slot % mine
    share = weights / jnp.sum(weights, axis=1, keepdims=True)
    spread = jnp.zeros((rows, slots), f32)
    for k in range(experts.shape[1]):
        spread = jnp.where(experts[:, k : k + 1] == expert, share[:, k : k + 1], spread)
    hits, rank = expert_hits(experts, expert)
    sender = slot % (2 * mine) // mine
    spread = jnp.where(rank == sender.astype(f32), spread, 0.0)
    slot_part = slot % per // (2 * mine)
    for p in range(parts):
        piece = jnp.where(slot_part == p, spread, 0.0)
        high = piece.astype(bf16)
        at = 2 * p * rows
        spread_ref[at : at + rows, :] = high
        spread_ref[at + rows : at + 2 * rows, :] = (piece - high.astype(f32)).astype(bf16)

    for copy in copies[2:6]:
        copy.wait()
    normed = normed_ref[...]
    shared_inner = (
        jax.nn.silu(dot(normed, shared_gate[...])) * dot(normed, shared_up[...])
    ).astype(bf16)
    lanes = mix.shape[1]
    logit = jnp.zeros((rows, lanes), f32)
    for i in range(width // lanes):
        logit = logit + normed[:, i * lanes : (i + 1) * lanes].astype(f32) * mix[
            i : i + 1, :
        ].astype(f32)
    scale = jax.nn.sigmoid(jnp.sum(logit, axis=-1, keepdims=True))
    base_ref[...] = hidden_ref[:, columns_at].astype(f32) + scale * dot(
        shared_inner, shared_down[...]
    )
    for copy in copies[6:]:
        copy.wait()


def expert_kernel(received, gate, up, down, sent_ref, taken, result):
    mine, width, inner_width = gate.shape
    slots, columns = received.shape
    parts = width // columns
    rows = slots // (parts * mine)
    half = width // 2
    groups = parts * mine
    block = 32
    inward = group_order(groups, block, True)
    outward = group_order(groups, block, False)

    for b in range(rows // block):
        ordered = dot(inward, received[b * groups * block : (b + 1) * groups * block, :]).astype(
            bf16
        )
        for p in range(parts):
            for j in range(mine):
                at = (p * mine + j) * block
                taken[j, b * block : (b + 1) * block, p * columns : (p + 1) * columns] = ordered[
                    at : at + block
                ]
    for j in range(mine):
        inner = (jax.nn.silu(dot(taken[j], gate[j])) * dot(taken[j], up[j])).astype(bf16)
        result[j] = dot(inner, down[j]).astype(bf16)

    n_dev = rows // 2
    for t in range(2):
        for b in range(n_dev // block):
            gathered = jnp.concatenate(
                [
                    result[
                        j,
                        s * n_dev + b * block : s * n_dev + (b + 1) * block,
                        t * half + p * columns : t * half + (p + 1) * columns,
                    ]
                    for p in range(half // columns)
                    for s in range(2)
                    for j in range(mine)
                ],
                axis=0,
            )
            at = (t * n_dev + b * block) * groups
            sent_ref[at : at + groups * block, :] = dot(outward, gathered).astype(bf16)


def combine_kernel(spread_ref, base_ref, returned, out_ref):
    rows, half = base_ref.shape
    columns = returned.shape[1]
    routed = dot(spread_ref[...], returned[...])
    for p in range(half // columns):
        at = 2 * p * rows
        value = routed[at : at + rows] + routed[at + rows : at + 2 * rows]
        out_ref[:, p * columns : (p + 1) * columns] = (
            base_ref[:, p * columns : (p + 1) * columns] + value
        ).astype(bf16)


VMEM = pl.BlockSpec(memory_space=pltpu.VMEM)
HBM = pl.BlockSpec(memory_space=pltpu.HBM)


def exchange(value):
    return lax.all_to_all(value, ("side", "dev"), split_axis=0, concat_axis=0, tiled=True)


def on_device(
    out_gates,
    queries,
    keys_new,
    values_new,
    lengths,
    page_table,
    cache_pool,
    query_gain,
    key_gain,
    out_weight,
    residual,
    post_gain,
    experts,
    route_weights,
    gate_weight,
    up_weight,
    down_weight,
    shared_gate,
    shared_up,
    shared_down,
    shared_mix,
):
    n_dev = lax.axis_size("dev")
    local, width, inner_width = gate_weight.shape
    rows = queries.shape[0]
    head = keys_new.shape[1]
    heads = width // head
    pages, page, both = cache_pool.shape
    tokens = pages * page
    mine = local // 2
    columns = width * mine // 8
    slots = 2 * n_dev * 8
    sources = (
        lengths[None, :],
        page_table.T,
        experts.T,
        queries,
        query_gain[None, :],
        keys_new,
        key_gain[None, :],
        values_new,
        out_gates,
        residual,
        post_gain[None, :],
        cache_pool.reshape(tokens, both),
        out_weight,
    )
    packed, hidden, normed = pl.pallas_call(
        functools.partial(front_kernel, page=page, local=local),
        out_shape=(
            jax.ShapeDtypeStruct((slots, columns), bf16),
            jax.ShapeDtypeStruct((rows, width), bf16),
            jax.ShapeDtypeStruct((rows, width), bf16),
        ),
        in_specs=[HBM] * len(sources),
        out_specs=(VMEM, VMEM, VMEM),
        scratch_shapes=[pltpu.VMEM(source.shape, source.dtype) for source in sources]
        + [
            pltpu.VMEM((heads * rows, head), bf16),
            pltpu.VMEM((heads * rows, tokens), bf16),
            pltpu.VMEM((rows, width), bf16),
            pltpu.SemaphoreType.DMA((18,)),
        ],
        compiler_params=pltpu.CompilerParams(vmem_limit_bytes=63 * MIB),
    )(*sources)
    received = exchange(packed)
    half = width // 2
    inner_width = gate_weight.shape[2]
    base, spread, gate, up, down = pl.pallas_call(
        functools.partial(middle_kernel, n_dev=n_dev),
        out_shape=(
            jax.ShapeDtypeStruct((rows, half), f32),
            jax.ShapeDtypeStruct((4 * rows, slots), bf16),
            jax.ShapeDtypeStruct((mine, width, inner_width), bf16),
            jax.ShapeDtypeStruct((mine, width, inner_width), bf16),
            jax.ShapeDtypeStruct((mine, inner_width, width), bf16),
        ),
        in_specs=[VMEM] * 2 + [HBM] * 9,
        out_specs=(VMEM,) * 5,
        scratch_shapes=[
            pltpu.VMEM(experts.T.shape, i32),
            pltpu.VMEM(route_weights.T.shape, f32),
            pltpu.VMEM((width // 128, 128), bf16),
            pltpu.VMEM(shared_gate.shape, bf16),
            pltpu.VMEM(shared_up.shape, bf16),
            pltpu.VMEM((shared_down.shape[0], half), bf16),
            pltpu.SemaphoreType.DMA((9,)),
        ],
        compiler_params=pltpu.CompilerParams(vmem_limit_bytes=44 * MIB),
        cost_estimate=pl.CostEstimate(
            flops=2 * rows * width * 3 * inner_width, bytes_accessed=10 * MIB, transcendentals=0
        ),
    )(
        normed,
        hidden,
        experts.T,
        route_weights.T,
        shared_mix.reshape(width // 128, 128),
        shared_gate,
        shared_up,
        shared_down,
        gate_weight,
        up_weight,
        down_weight,
    )
    sent = pl.pallas_call(
        expert_kernel,
        out_shape=jax.ShapeDtypeStruct((slots, columns), bf16),
        in_specs=[VMEM] * 4,
        out_specs=VMEM,
        scratch_shapes=[
            pltpu.VMEM((mine, 2 * n_dev, width), bf16),
            pltpu.VMEM((mine, 2 * n_dev, width), bf16),
        ],
        compiler_params=pltpu.CompilerParams(vmem_limit_bytes=32 * MIB),
    )(received, gate, up, down)
    returned = exchange(sent)
    return pl.pallas_call(
        combine_kernel,
        out_shape=jax.ShapeDtypeStruct((rows, half), bf16),
        in_specs=[VMEM] * 3,
        out_specs=VMEM,
        compiler_params=pltpu.CompilerParams(vmem_limit_bytes=8 * MIB),
    )(spread, base, returned)


def solution(mesh):
    placed = (
        P("dev", None),
        P("dev", None),
        P("dev", None),
        P("dev", None),
        P("dev"),
        P("dev", None),
        P("dev", None, None),
        P(),
        P(),
        P(),
        P("dev", None),
        P(),
        P("dev", None),
        P("dev", None),
        P("dev", None, None),
        P("dev", None, None),
        P("dev", None, None),
        P(),
        P(),
        P(),
        P(),
    )
    return jax.shard_map(
        on_device, mesh=mesh, in_specs=placed, out_specs=P("dev", "side"), check_vma=False
    )
```

```python
import functools
import jax
import jax.numpy as jnp
from jax import lax
from jax.experimental import pallas as pl
from jax.experimental.pallas import tpu as pltpu
from jax.sharding import PartitionSpec as P

eps = 1e-06
f32 = jnp.float32
bf16 = jnp.bfloat16
i32 = jnp.int32
MIB = 1 << 20


def dot(left, right):
    return jnp.dot(left, right, preferred_element_type=f32)


def iota(shape, axis):
    return lax.broadcasted_iota(i32, shape, axis)


def rms_scale(wide, gain):
    return wide * lax.rsqrt(jnp.mean(wide * wide, axis=-1, keepdims=True) + eps) * gain


def group_order(groups, members, to_groups):
    size = groups * members
    by_group = iota((size, size), 0 if to_groups else 1)
    by_member = iota((size, size), 1 if to_groups else 0)
    wanted = (by_group % members) * groups + by_group // members
    return (wanted == by_member).astype(f32).astype(bf16)


def expert_hits(experts, slot_expert):
    rows, topk = experts.shape
    hits = jnp.zeros(slot_expert.shape, f32)
    for k in range(topk):
        hits = jnp.where(experts[:, k : k + 1] == slot_expert, 1.0, hits)
    earlier = (iota((rows, rows), 1) < iota((rows, rows), 0)).astype(f32).astype(bf16)
    rank = dot(earlier, hits.astype(bf16))
    return hits, rank


def start_all(pairs, sem):
    copies = [
        pltpu.make_async_copy(source, target, sem.at[i]) for i, (source, target) in enumerate(pairs)
    ]
    for copy in copies:
        copy.start()
    return copies


def pieces_of(source, target, count):
    size = source.shape[0] // count
    return [
        (source.at[pl.ds(i * size, size)], target.at[pl.ds(i * size, size)]) for i in range(count)
    ]


def front_kernel(*refs, page, local):
    sources, refs = refs[:12], refs[12:]
    packed_ref, hidden_ref, attended, refs = *refs[:3], refs[3:]
    targets, refs = refs[:12], refs[12:]
    query, prob, valid, chosen, sem = refs
    residual_hbm, pool_hbm, weight_hbm = sources[-3:]
    (
        lengths_ref,
        table_in,
        experts_in,
        queries_ref,
        query_gain_ref,
        keys_ref,
        key_gain_ref,
        values_ref,
        gates_ref,
        residual_ref,
        pool,
        weight,
    ) = targets
    rows, width = queries_ref.shape
    half = width // 2
    head = keys_ref.shape[1]
    heads = width // head
    tokens = pool.shape[0]
    context = 256
    chunks = tokens // context
    weight_parts = 4
    quarter = width // weight_parts
    side = lax.axis_index("side")
    columns_at = pl.ds(pl.multiple_of(side * half, half), half)
    pairs = list(zip(sources, targets))
    copies = start_all(
        pairs[:7]
        + pieces_of(pool_hbm, pool, chunks)
        + pairs[7:9]
        + [(residual_hbm.at[:, columns_at], residual_ref)]
        + [
            (source.at[:, columns_at], target)
            for source, target in pieces_of(weight_hbm, weight, weight_parts)
        ],
        sem,
    )
    pool_copies = copies[7 : 7 + chunks]
    late_copies = copies[7 + chunks : 10 + chunks]
    weight_copies = copies[10 + chunks :]
    for copy in copies[:7]:
        copy.wait()

    slots, columns = packed_ref.shape
    parts = half // columns
    mine = local // 2
    slot = iota((rows, slots), 1)
    per = parts * 2 * mine
    destination = slot // per
    n_dev = slots // per // 2
    expert = (destination % n_dev) * local + (destination // n_dev) * mine + slot % mine
    hits, rank = expert_hits(experts_in[...].T, expert)
    slot_rank = slot % (2 * mine) // mine
    picked = jnp.where(rank == slot_rank.astype(f32), hits, 0.0)
    slot_part = slot % per // (2 * mine)
    picked = jnp.concatenate(
        [jnp.where(slot_part == p, picked, 0.0) for p in range(parts)], axis=0
    )
    chosen[...] = picked.T.astype(bf16)

    table = table_in[...].T
    same = iota((rows, rows), 0) == iota((rows, rows), 1)
    lengths = jnp.sum(
        jnp.where(same, jnp.broadcast_to(lengths_ref[...], (rows, rows)), 0), axis=1, keepdims=True
    )
    for c in range(chunks):
        token = iota((rows, context), 1) + c * context
        token_page = token // page
        token_in = token % page
        mask = jnp.zeros((rows, context), f32)
        for entry in range(table.shape[1]):
            hit = (table[:, entry : entry + 1] == token_page) & (
                token_in + entry * page < lengths
            )
            mask = jnp.where(hit, 1.0, mask)
        valid[:, c * context : (c + 1) * context] = mask

    scale = head ** (-0.5)
    key_normed = rms_scale(keys_ref[...].astype(f32), key_gain_ref[...]).astype(bf16).astype(f32)
    own = []
    for h in range(heads):
        part = queries_ref[:, h * head : (h + 1) * head].astype(f32)
        normed = rms_scale(part, query_gain_ref[...]).astype(bf16)
        query[h * rows : (h + 1) * rows, :] = normed
        own.append(jnp.sum(normed.astype(f32) * key_normed, axis=-1, keepdims=True))
    own_weight = jnp.exp(jnp.concatenate(own, axis=0) * scale)

    total = jnp.zeros((heads * rows, context), f32)
    for c in range(chunks):
        pool_copies[c].wait()
        at = slice(c * context, (c + 1) * context)
        scores = lax.dot_general(
            query[...],
            pool[at, :head],
            (((1,), (1,)), ((), ())),
            preferred_element_type=f32,
        )
        weights = jnp.exp(scores * scale)
        weights = (weights.reshape(heads, rows, context) * valid[:, at][None]).reshape(
            heads * rows, context
        )
        total = total + weights
        prob[:, at] = weights.astype(bf16)
    mixed = dot(prob[...], pool[:, head:])
    for copy in late_copies:
        copy.wait()
    inverse = 1.0 / (jnp.sum(total, axis=1, keepdims=True) + own_weight)
    new_values = values_ref[...].astype(f32)
    for h in range(heads):
        part = slice(h * rows, (h + 1) * rows)
        value = (mixed[part] + own_weight[part] * new_values) * inverse[part]
        gate = jax.nn.sigmoid(gates_ref[:, h * head : (h + 1) * head].astype(f32))
        attended[:, h * head : (h + 1) * head] = (value * gate).astype(bf16)

    projected = residual_ref[...].astype(f32)
    for i, copy in enumerate(weight_copies):
        copy.wait()
        at = slice(i * quarter, (i + 1) * quarter)
        projected = projected + dot(attended[:, at], weight[at, :])
    hidden = projected.astype(bf16)
    hidden_ref[...] = hidden
    stacked = jnp.concatenate(
        [hidden[:, p * columns : (p + 1) * columns] for p in range(parts)], axis=0
    )
    packed_ref[...] = dot(chosen[...], stacked).astype(bf16)


def middle_kernel(*refs, n_dev):
    (
        attended,
        hidden_ref,
        experts_hbm,
        weights_hbm,
        mix_hbm,
        residual_hbm,
        post_gain_hbm,
        out_weight_hbm,
        shared_gate_hbm,
        shared_up_hbm,
        shared_down_hbm,
        gate_hbm,
        up_hbm,
        down_hbm,
    ) = refs[:14]
    base_ref, spread_ref, post_gain, gate_ref, up_ref, down_ref = refs[14:20]
    (
        experts_in,
        weights_in,
        mix,
        residual,
        out_weight,
        shared_gate,
        shared_up,
        shared_down,
        hidden,
        sem,
    ) = refs[20:]
    rows, width = hidden.shape
    half = width // 2
    local = gate_hbm.shape[0]
    mine = local // 2
    side = lax.axis_index("side")
    experts_at = pl.ds(side * mine, mine)
    columns_at = pl.ds(pl.multiple_of(side * half, half), half)
    others_at = pl.ds(pl.multiple_of((1 - side) * half, half), half)
    copies = start_all(
        [
            (experts_hbm, experts_in),
            (weights_hbm, weights_in),
            (mix_hbm, mix),
            (residual_hbm.at[:, others_at], residual),
            (post_gain_hbm, post_gain),
            (out_weight_hbm.at[:, others_at], out_weight),
            (shared_gate_hbm, shared_gate),
            (shared_up_hbm, shared_up),
            (shared_down_hbm.at[:, columns_at], shared_down),
            (gate_hbm.at[experts_at], gate_ref),
            (up_hbm.at[experts_at], up_ref),
            (down_hbm.at[experts_at], down_ref),
        ],
        sem,
    )
    for copy in copies[:2]:
        copy.wait()
    experts = experts_in[...].T
    weights = weights_in[...].T
    slots = spread_ref.shape[1]
    per = slots // (2 * n_dev)
    parts = per // local
    slot = iota((rows, slots), 1)
    source = slot // per
    expert = (source % n_dev) * local + (source // n_dev) * mine + slot % mine
    share = weights / jnp.sum(weights, axis=1, keepdims=True)
    spread = jnp.zeros((rows, slots), f32)
    for k in range(experts.shape[1]):
        spread = jnp.where(experts[:, k : k + 1] == expert, share[:, k : k + 1], spread)
    hits, rank = expert_hits(experts, expert)
    slot_rank = slot % (2 * mine) // mine
    spread = jnp.where(rank == slot_rank.astype(f32), spread, 0.0)
    slot_part = slot % per // (2 * mine)
    for p in range(parts):
        piece = jnp.where(slot_part == p, spread, 0.0)
        high = piece.astype(bf16)
        at = 2 * p * rows
        spread_ref[at : at + rows, :] = high
        spread_ref[at + rows : at + 2 * rows, :] = (piece - high.astype(f32)).astype(bf16)

    for copy in copies[2:9]:
        copy.wait()
    mine_hidden = hidden_ref[...]
    hidden[:, columns_at] = mine_hidden
    hidden[:, others_at] = (
        residual[...].astype(f32) + dot(attended[...], out_weight[...])
    ).astype(bf16)
    normed = rms_scale(hidden[...].astype(f32), post_gain[...]).astype(bf16)
    shared_inner = (
        jax.nn.silu(dot(normed, shared_gate[...])) * dot(normed, shared_up[...])
    ).astype(bf16)
    lanes = mix.shape[1]
    logit = jnp.zeros((rows, lanes), f32)
    for i in range(width // lanes):
        logit = logit + normed[:, i * lanes : (i + 1) * lanes].astype(f32) * mix[
            i : i + 1, :
        ].astype(f32)
    scale = jax.nn.sigmoid(jnp.sum(logit, axis=-1, keepdims=True))
    base_ref[...] = mine_hidden.astype(f32) + scale * dot(shared_inner, shared_down[...])
    for copy in copies[9:]:
        copy.wait()


def expert_kernel(received, post_gain, gate, up, down, sent_ref, taken, result):
    mine, width, inner_width = gate.shape
    slots, columns = received.shape
    half = width // 2
    parts = half // columns
    groups = parts * 2 * mine
    n_dev = slots // groups // 2
    block = 32
    inward = group_order(groups, block, True)
    outward = group_order(groups, block, False)

    for s in range(2):
        for b in range(n_dev // block):
            at = (s * n_dev + b * block) * groups
            ordered = dot(inward, received[at : at + groups * block, :]).astype(bf16)
            for p in range(parts):
                for r in range(2):
                    for j in range(mine):
                        at = ((p * 2 + r) * mine + j) * block
                        row = r * n_dev + b * block
                        column = s * half + p * columns
                        taken[j, row : row + block, column : column + columns] = ordered[
                            at : at + block
                        ]
    for j in range(mine):
        normed = rms_scale(taken[j].astype(f32), post_gain[...]).astype(bf16)
        inner = (jax.nn.silu(dot(normed, gate[j])) * dot(normed, up[j])).astype(bf16)
        result[j] = dot(inner, down[j]).astype(bf16)

    for t in range(2):
        for b in range(n_dev // block):
            gathered = jnp.concatenate(
                [
                    result[
                        j,
                        r * n_dev + b * block : r * n_dev + (b + 1) * block,
                        t * half + p * columns : t * half + (p + 1) * columns,
                    ]
                    for p in range(parts)
                    for r in range(2)
                    for j in range(mine)
                ],
                axis=0,
            )
            at = (t * n_dev + b * block) * groups
            sent_ref[at : at + groups * block, :] = dot(outward, gathered).astype(bf16)


def combine_kernel(spread_ref, base_ref, returned, out_ref):
    rows, half = base_ref.shape
    columns = returned.shape[1]
    routed = dot(spread_ref[...], returned[...])
    for p in range(half // columns):
        at = 2 * p * rows
        value = routed[at : at + rows] + routed[at + rows : at + 2 * rows]
        out_ref[:, p * columns : (p + 1) * columns] = (
            base_ref[:, p * columns : (p + 1) * columns] + value
        ).astype(bf16)


VMEM = pl.BlockSpec(memory_space=pltpu.VMEM)
HBM = pl.BlockSpec(memory_space=pltpu.HBM)


def exchange(value):
    return lax.all_to_all(value, ("side", "dev"), split_axis=0, concat_axis=0, tiled=True)


def on_device(
    out_gates,
    queries,
    keys_new,
    values_new,
    lengths,
    page_table,
    cache_pool,
    query_gain,
    key_gain,
    out_weight,
    residual,
    post_gain,
    experts,
    route_weights,
    gate_weight,
    up_weight,
    down_weight,
    shared_gate,
    shared_up,
    shared_down,
    shared_mix,
):
    n_dev = lax.axis_size("dev")
    local, width, inner_width = gate_weight.shape
    rows = queries.shape[0]
    head = keys_new.shape[1]
    heads = width // head
    pages, page, both = cache_pool.shape
    tokens = pages * page
    mine = local // 2
    columns = width * mine // 8
    slots = 2 * n_dev * 8
    half = width // 2
    inner_width = gate_weight.shape[2]
    sources = (
        lengths[None, :],
        page_table.T,
        experts.T,
        queries,
        query_gain[None, :],
        keys_new,
        key_gain[None, :],
        values_new,
        out_gates,
        residual,
        cache_pool.reshape(tokens, both),
        out_weight,
    )
    held = [pltpu.VMEM(source.shape, source.dtype) for source in sources]
    held[9] = pltpu.VMEM((rows, half), bf16)
    held[11] = pltpu.VMEM((width, half), bf16)
    packed, hidden, attended = pl.pallas_call(
        functools.partial(front_kernel, page=page, local=local),
        out_shape=(
            jax.ShapeDtypeStruct((slots, columns), bf16),
            jax.ShapeDtypeStruct((rows, half), bf16),
            jax.ShapeDtypeStruct((rows, width), bf16),
        ),
        in_specs=[HBM] * len(sources),
        out_specs=(VMEM, VMEM, VMEM),
        scratch_shapes=held
        + [
            pltpu.VMEM((heads * rows, head), bf16),
            pltpu.VMEM((heads * rows, tokens), bf16),
            pltpu.VMEM((rows, tokens), f32),
            pltpu.VMEM((slots, half // columns * rows), bf16),
            pltpu.SemaphoreType.DMA((14 + tokens // 256,)),
        ],
        compiler_params=pltpu.CompilerParams(vmem_limit_bytes=63 * MIB),
    )(*sources)
    received = exchange(packed)
    base, spread, gain, gate, up, down = pl.pallas_call(
        functools.partial(middle_kernel, n_dev=n_dev),
        out_shape=(
            jax.ShapeDtypeStruct((rows, half), f32),
            jax.ShapeDtypeStruct((4 * rows, slots), bf16),
            jax.ShapeDtypeStruct((1, width), f32),
            jax.ShapeDtypeStruct((mine, width, inner_width), bf16),
            jax.ShapeDtypeStruct((mine, width, inner_width), bf16),
            jax.ShapeDtypeStruct((mine, inner_width, width), bf16),
        ),
        in_specs=[VMEM] * 2 + [HBM] * 12,
        out_specs=(VMEM,) * 6,
        scratch_shapes=[
            pltpu.VMEM(experts.T.shape, i32),
            pltpu.VMEM(route_weights.T.shape, f32),
            pltpu.VMEM((width // 128, 128), bf16),
            pltpu.VMEM((rows, half), bf16),
            pltpu.VMEM((width, half), bf16),
            pltpu.VMEM(shared_gate.shape, bf16),
            pltpu.VMEM(shared_up.shape, bf16),
            pltpu.VMEM((shared_down.shape[0], half), bf16),
            pltpu.VMEM((rows, width), bf16),
            pltpu.SemaphoreType.DMA((12,)),
        ],
        compiler_params=pltpu.CompilerParams(vmem_limit_bytes=40 * MIB),
        cost_estimate=pl.CostEstimate(
            flops=2 * rows * width * (half + 3 * inner_width),
            bytes_accessed=14 * MIB,
            transcendentals=0,
        ),
    )(
        attended,
        hidden,
        experts.T,
        route_weights.T,
        shared_mix.reshape(width // 128, 128),
        residual,
        post_gain[None, :],
        out_weight,
        shared_gate,
        shared_up,
        shared_down,
        gate_weight,
        up_weight,
        down_weight,
    )
    sent = pl.pallas_call(
        expert_kernel,
        out_shape=jax.ShapeDtypeStruct((slots, columns), bf16),
        in_specs=[VMEM] * 5,
        out_specs=VMEM,
        scratch_shapes=[
            pltpu.VMEM((mine, 2 * n_dev, width), bf16),
            pltpu.VMEM((mine, 2 * n_dev, width), bf16),
        ],
        compiler_params=pltpu.CompilerParams(vmem_limit_bytes=24 * MIB),
    )(received, gain, gate, up, down)
    returned = exchange(sent)
    return pl.pallas_call(
        combine_kernel,
        out_shape=jax.ShapeDtypeStruct((rows, half), bf16),
        in_specs=[VMEM] * 3,
        out_specs=VMEM,
        compiler_params=pltpu.CompilerParams(vmem_limit_bytes=8 * MIB),
    )(spread, base, returned)


def solution(mesh):
    placed = (
        P("dev", None),
        P("dev", None),
        P("dev", None),
        P("dev", None),
        P("dev"),
        P("dev", None),
        P("dev", None, None),
        P(),
        P(),
        P(),
        P("dev", None),
        P(),
        P("dev", None),
        P("dev", None),
        P("dev", None, None),
        P("dev", None, None),
        P("dev", None, None),
        P(),
        P(),
        P(),
        P(),
    )
    return jax.shard_map(
        on_device, mesh=mesh, in_specs=placed, out_specs=P("dev", "side"), check_vma=False
    )
```

```python
import functools
import jax
import jax.numpy as jnp
from jax import lax
from jax.experimental import pallas as pl
from jax.experimental.pallas import tpu as pltpu
from jax.sharding import PartitionSpec as P

eps = 1e-06
f32 = jnp.float32
bf16 = jnp.bfloat16
i32 = jnp.int32
MIB = 1 << 20


def dot(left, right):
    return jnp.dot(left, right, preferred_element_type=f32)


def iota(shape, axis):
    return lax.broadcasted_iota(i32, shape, axis)


def rms_scale(wide, gain):
    return wide * lax.rsqrt(jnp.mean(wide * wide, axis=-1, keepdims=True) + eps) * gain


def group_order(groups, members, to_groups):
    size = groups * members
    by_group = iota((size, size), 0 if to_groups else 1)
    by_member = iota((size, size), 1 if to_groups else 0)
    wanted = (by_group % members) * groups + by_group // members
    return (wanted == by_member).astype(f32).astype(bf16)


def expert_hits(experts, slot_expert):
    rows, topk = experts.shape
    hits = jnp.zeros((rows, slot_expert.shape[1]), f32)
    for k in range(topk):
        hits = jnp.where(experts[:, k : k + 1] == slot_expert, 1.0, hits)
    earlier = (iota((rows, rows), 1) < iota((rows, rows), 0)).astype(f32).astype(bf16)
    rank = dot(earlier, hits.astype(bf16))
    return hits, rank


def start_all(pairs, sem):
    copies = [
        pltpu.make_async_copy(source, target, sem.at[i]) for i, (source, target) in enumerate(pairs)
    ]
    for copy in copies:
        copy.start()
    return copies


def pieces_of(source, target, count):
    size = source.shape[0] // count
    return [
        (source.at[pl.ds(i * size, size)], target.at[pl.ds(i * size, size)]) for i in range(count)
    ]


def front_kernel(*refs, page, local):
    sources, refs = refs[:12], refs[12:]
    packed_ref, hidden_ref, attended, refs = *refs[:3], refs[3:]
    targets, refs = refs[:12], refs[12:]
    query, prob, valid, chosen, sem = refs
    residual_hbm, pool_hbm, weight_hbm = sources[-3:]
    (
        lengths_ref,
        table_in,
        experts_in,
        queries_ref,
        query_gain_ref,
        keys_ref,
        key_gain_ref,
        values_ref,
        gates_ref,
        residual_ref,
        pool,
        weight,
    ) = targets
    rows, width = queries_ref.shape
    half = width // 2
    head = keys_ref.shape[1]
    heads = width // head
    tokens = pool.shape[0]
    context = 256
    chunks = tokens // context
    weight_parts = 4
    quarter = width // weight_parts
    side = lax.axis_index("side")
    columns_at = pl.ds(pl.multiple_of(side * half, half), half)
    pairs = list(zip(sources, targets))
    copies = start_all(
        pairs[:7]
        + [pairs[10]]
        + pairs[7:9]
        + [
            (residual_hbm.at[:, columns_at], residual_ref),
        ]
        + [
            (source.at[:, columns_at], target)
            for source, target in pieces_of(weight_hbm, weight, weight_parts)
        ],
        sem,
    )
    for copy in copies[:7]:
        copy.wait()

    table = table_in[...].T
    same = iota((rows, rows), 0) == iota((rows, rows), 1)
    lengths = jnp.sum(
        jnp.where(same, jnp.broadcast_to(lengths_ref[...], (rows, rows)), 0), axis=1, keepdims=True
    )
    pages = tokens // page
    number = iota((1, pages), 1)
    limit = jnp.zeros((rows, pages), i32)
    for entry in range(table.shape[1]):
        held = jnp.clip(lengths - entry * page, 0, page)
        limit = jnp.where(table[:, entry : entry + 1] == number, jnp.maximum(limit, held), limit)
    per_chunk = context // page
    limit = limit.astype(f32).astype(bf16)
    limit = jnp.concatenate(
        [limit[:, c * per_chunk : (c + 1) * per_chunk] for c in range(chunks)], axis=0
    )
    expand = iota((per_chunk, context), 1) // page == iota((per_chunk, context), 0)
    limit = dot(limit, expand.astype(f32).astype(bf16))
    valid[...] = (iota((1, context), 1) % page < limit.astype(i32)).astype(f32)

    scale = head ** (-0.5)
    key_normed = rms_scale(keys_ref[...].astype(f32), key_gain_ref[...]).astype(bf16).astype(f32)
    own = []
    for h in range(heads):
        part = queries_ref[:, h * head : (h + 1) * head].astype(f32)
        normed = rms_scale(part, query_gain_ref[...]).astype(bf16)
        query[h * rows : (h + 1) * rows, :] = normed * jnp.asarray(scale, bf16)
        own.append(jnp.sum(normed.astype(f32) * key_normed, axis=-1, keepdims=True))
    own_weight = jnp.exp(jnp.concatenate(own, axis=0) * scale)

    for copy in copies[7:11]:
        copy.wait()
    total = jnp.zeros((heads * rows, context), f32)
    for c in range(chunks):
        at = slice(c * context, (c + 1) * context)
        scores = lax.dot_general(
            query[...],
            pool[at, :head],
            (((1,), (1,)), ((), ())),
            preferred_element_type=f32,
        )
        mask = valid[c * rows : (c + 1) * rows, :]
        weights = (jnp.exp(scores).reshape(heads, rows, context) * mask[None]).reshape(
            heads * rows, context
        )
        total = total + weights
        prob[:, at] = weights.astype(bf16)

    slots, columns = packed_ref.shape
    parts = half // columns
    mine = local // 2
    slot = iota((1, slots), 1)
    per = parts * 2 * mine
    destination = slot // per
    n_dev = slots // per // 2
    expert = (destination % n_dev) * local + (destination // n_dev) * mine + slot % mine
    hits, rank = expert_hits(experts_in[...].T, expert)
    slot_rank = (slot % (2 * mine) // mine).astype(f32)
    picked = jnp.where(rank == slot_rank, hits, 0.0)
    slot_part = slot % per // (2 * mine)
    picked = jnp.concatenate(
        [jnp.where(slot_part == p, picked, 0.0) for p in range(parts)], axis=0
    )
    chosen[...] = picked.T.astype(bf16)

    mixed = dot(prob[...], pool[:, head:])
    inverse = 1.0 / (jnp.sum(total, axis=1, keepdims=True) + own_weight)
    new_values = values_ref[...].astype(f32)
    for h in range(heads):
        part = slice(h * rows, (h + 1) * rows)
        value = (mixed[part] + own_weight[part] * new_values) * inverse[part]
        gate = jax.nn.sigmoid(gates_ref[:, h * head : (h + 1) * head].astype(f32))
        attended[:, h * head : (h + 1) * head] = (value * gate).astype(bf16)

    projected = residual_ref[...].astype(f32)
    for i, copy in enumerate(copies[11:]):
        copy.wait()
        at = slice(i * quarter, (i + 1) * quarter)
        projected = projected + dot(attended[:, at], weight[at, :])
    hidden = projected.astype(bf16)
    hidden_ref[...] = hidden
    stacked = jnp.concatenate(
        [hidden[:, p * columns : (p + 1) * columns] for p in range(parts)], axis=0
    )
    packed_ref[...] = dot(chosen[...], stacked).astype(bf16)


def middle_kernel(*refs, n_dev):
    (
        attended,
        hidden_ref,
        experts_hbm,
        weights_hbm,
        mix_hbm,
        residual_hbm,
        post_gain_hbm,
        out_weight_hbm,
        shared_gate_hbm,
        shared_up_hbm,
        shared_down_hbm,
        gate_hbm,
        up_hbm,
    ) = refs[:13]
    base_ref, spread_ref, post_gain, first_ref = refs[13:17]
    (
        experts_in,
        weights_in,
        mix,
        residual,
        out_weight,
        shared_gate,
        shared_up,
        shared_down,
        hidden,
        sem,
    ) = refs[17:]
    rows, width = hidden.shape
    half = width // 2
    local = gate_hbm.shape[0]
    mine = local // 2
    side = lax.axis_index("side")
    columns_at = pl.ds(pl.multiple_of(side * half, half), half)
    others_at = pl.ds(pl.multiple_of((1 - side) * half, half), half)
    copies = start_all(
        [
            (experts_hbm, experts_in),
            (weights_hbm, weights_in),
            (mix_hbm, mix),
            (residual_hbm.at[:, others_at], residual),
            (post_gain_hbm, post_gain),
            (out_weight_hbm.at[:, others_at], out_weight),
            (shared_gate_hbm, shared_gate),
            (shared_up_hbm, shared_up),
            (shared_down_hbm.at[:, columns_at], shared_down),
            (gate_hbm.at[side * mine], first_ref.at[0]),
            (up_hbm.at[side * mine], first_ref.at[1]),
        ],
        sem,
    )
    for copy in copies[:2]:
        copy.wait()
    experts = experts_in[...].T
    weights = weights_in[...].T
    slots = spread_ref.shape[1]
    per = slots // (2 * n_dev)
    parts = per // local
    slot = iota((1, slots), 1)
    source = slot // per
    expert = (source % n_dev) * local + (source // n_dev) * mine + slot % mine
    share = weights / jnp.sum(weights, axis=1, keepdims=True)
    spread = jnp.zeros((rows, slots), f32)
    for k in range(experts.shape[1]):
        spread = jnp.where(experts[:, k : k + 1] == expert, share[:, k : k + 1], spread)
    hits, rank = expert_hits(experts, expert)
    slot_rank = slot % (2 * mine) // mine
    spread = jnp.where(rank == slot_rank.astype(f32), spread, 0.0)
    slot_part = slot % per // (2 * mine)
    for p in range(parts):
        piece = jnp.where(slot_part == p, spread, 0.0)
        high = piece.astype(bf16)
        at = 2 * p * rows
        spread_ref[at : at + rows, :] = high
        spread_ref[at + rows : at + 2 * rows, :] = (piece - high.astype(f32)).astype(bf16)

    for copy in copies[2:9]:
        copy.wait()
    mine_hidden = hidden_ref[...]
    hidden[:, columns_at] = mine_hidden
    hidden[:, others_at] = (
        residual[...].astype(f32) + dot(attended[...], out_weight[...])
    ).astype(bf16)
    normed = rms_scale(hidden[...].astype(f32), post_gain[...]).astype(bf16)
    shared_inner = (
        jax.nn.silu(dot(normed, shared_gate[...])) * dot(normed, shared_up[...])
    ).astype(bf16)
    lanes = mix.shape[1]
    logit = jnp.zeros((rows, lanes), f32)
    for i in range(width // lanes):
        logit = logit + normed[:, i * lanes : (i + 1) * lanes].astype(f32) * mix[
            i : i + 1, :
        ].astype(f32)
    scale = jax.nn.sigmoid(jnp.sum(logit, axis=-1, keepdims=True))
    base_ref[...] = mine_hidden.astype(f32) + scale * dot(shared_inner, shared_down[...])
    for copy in copies[9:]:
        copy.wait()


def expert_kernel(
    received,
    post_gain,
    first,
    gate_hbm,
    up_hbm,
    down_hbm,
    sent_ref,
    gate,
    up,
    down,
    taken,
    result,
    sem,
):
    mine, inner_width, width = down.shape
    at = lax.axis_index("side") * mine
    copies = start_all(
        [
            pair
            for j in range(mine)
            for pair in (
                ((gate_hbm.at[at + j], gate.at[j - 1]), (up_hbm.at[at + j], up.at[j - 1]))
                if j
                else ()
            )
        ]
        + [(down_hbm.at[at + j], down.at[j]) for j in range(mine)],
        sem,
    )
    slots, columns = received.shape
    half = width // 2
    parts = half // columns
    groups = parts * 2 * mine
    n_dev = slots // groups // 2
    block = 32
    inward = group_order(groups, block, True)
    outward = group_order(groups, block, False)

    for s in range(2):
        for b in range(n_dev // block):
            at = (s * n_dev + b * block) * groups
            ordered = dot(inward, received[at : at + groups * block, :]).astype(bf16)
            for p in range(parts):
                for r in range(2):
                    for j in range(mine):
                        at = ((p * 2 + r) * mine + j) * block
                        row = r * n_dev + b * block
                        column = s * half + p * columns
                        taken[j, row : row + block, column : column + columns] = ordered[
                            at : at + block
                        ]
    inner = []
    for j in range(mine):
        normed = rms_scale(taken[j].astype(f32), post_gain[...]).astype(bf16)
        if j:
            copies[2 * j - 2].wait()
            copies[2 * j - 1].wait()
        gate_j, up_j = (gate[j - 1], up[j - 1]) if j else (first[0], first[1])
        inner.append((jax.nn.silu(dot(normed, gate_j)) * dot(normed, up_j)).astype(bf16))
    for j in range(mine):
        copies[2 * mine - 2 + j].wait()
        result[j] = dot(inner[j], down[j]).astype(bf16)

    for t in range(2):
        for b in range(n_dev // block):
            gathered = jnp.concatenate(
                [
                    result[
                        j,
                        r * n_dev + b * block : r * n_dev + (b + 1) * block,
                        t * half + p * columns : t * half + (p + 1) * columns,
                    ]
                    for p in range(parts)
                    for r in range(2)
                    for j in range(mine)
                ],
                axis=0,
            )
            at = (t * n_dev + b * block) * groups
            sent_ref[at : at + groups * block, :] = dot(outward, gathered).astype(bf16)


def combine_kernel(spread_ref, base_ref, returned, out_ref):
    rows, half = base_ref.shape
    columns = returned.shape[1]
    routed = dot(spread_ref[...], returned[...])
    for p in range(half // columns):
        at = 2 * p * rows
        value = routed[at : at + rows] + routed[at + rows : at + 2 * rows]
        out_ref[:, p * columns : (p + 1) * columns] = (
            base_ref[:, p * columns : (p + 1) * columns] + value
        ).astype(bf16)


VMEM = pl.BlockSpec(memory_space=pltpu.VMEM)
HBM = pl.BlockSpec(memory_space=pltpu.HBM)


def in_hbm(value):
    return pltpu.with_memory_space_constraint(value, pltpu.HBM)


def exchange(value):
    return lax.all_to_all(value, ("side", "dev"), split_axis=0, concat_axis=0, tiled=True)


def on_device(
    out_gates,
    queries,
    keys_new,
    values_new,
    lengths,
    page_table,
    cache_pool,
    query_gain,
    key_gain,
    out_weight,
    residual,
    post_gain,
    experts,
    route_weights,
    gate_weight,
    up_weight,
    down_weight,
    shared_gate,
    shared_up,
    shared_down,
    shared_mix,
):
    n_dev = lax.axis_size("dev")
    local, width, inner_width = gate_weight.shape
    rows = queries.shape[0]
    head = keys_new.shape[1]
    heads = width // head
    pages, page, both = cache_pool.shape
    tokens = pages * page
    mine = local // 2
    columns = width * mine // 8
    slots = 2 * n_dev * 8
    half = width // 2
    inner_width = gate_weight.shape[2]
    sources = (
        lengths[None, :],
        page_table.T,
        experts.T,
        queries,
        query_gain[None, :],
        keys_new,
        key_gain[None, :],
        values_new,
        out_gates,
        residual,
        cache_pool.reshape(tokens, both),
        out_weight,
    )
    held = [pltpu.VMEM(source.shape, source.dtype) for source in sources]
    held[9] = pltpu.VMEM((rows, half), bf16)
    held[11] = pltpu.VMEM((width, half), bf16)
    packed, hidden, attended = pl.pallas_call(
        functools.partial(front_kernel, page=page, local=local),
        out_shape=(
            pltpu.VMEM((slots, columns), bf16),
            jax.ShapeDtypeStruct((rows, half), bf16),
            jax.ShapeDtypeStruct((rows, width), bf16),
        ),
        in_specs=[HBM] * len(sources),
        out_specs=(VMEM, VMEM, VMEM),
        scratch_shapes=held
        + [
            pltpu.VMEM((heads * rows, head), bf16),
            pltpu.VMEM((heads * rows, tokens), bf16),
            pltpu.VMEM((rows * tokens // 256, 256), f32),
            pltpu.VMEM((slots, half // columns * rows), bf16),
            pltpu.SemaphoreType.DMA((15,)),
        ],
        compiler_params=pltpu.CompilerParams(vmem_limit_bytes=32 * MIB),
    )(*map(in_hbm, sources))
    received = exchange(packed)
    base, spread, gain, first = pl.pallas_call(
        functools.partial(middle_kernel, n_dev=n_dev),
        out_shape=(
            jax.ShapeDtypeStruct((rows, half), f32),
            jax.ShapeDtypeStruct((4 * rows, slots), bf16),
            jax.ShapeDtypeStruct((1, width), f32),
            jax.ShapeDtypeStruct((2, width, inner_width), bf16),
        ),
        in_specs=[VMEM] * 2 + [HBM] * 11,
        out_specs=(VMEM,) * 4,
        scratch_shapes=[
            pltpu.VMEM(experts.T.shape, i32),
            pltpu.VMEM(route_weights.T.shape, f32),
            pltpu.VMEM((width // 128, 128), bf16),
            pltpu.VMEM((rows, half), bf16),
            pltpu.VMEM((width, half), bf16),
            pltpu.VMEM(shared_gate.shape, bf16),
            pltpu.VMEM(shared_up.shape, bf16),
            pltpu.VMEM((shared_down.shape[0], half), bf16),
            pltpu.VMEM((rows, width), bf16),
            pltpu.SemaphoreType.DMA((11,)),
        ],
        compiler_params=pltpu.CompilerParams(vmem_limit_bytes=24 * MIB),
        cost_estimate=pl.CostEstimate(
            flops=2 * rows * width * (half + 3 * inner_width),
            bytes_accessed=10 * MIB,
            transcendentals=0,
        ),
    )(
        attended,
        hidden,
        *map(
            in_hbm,
            (
                experts.T,
                route_weights.T,
                shared_mix.reshape(width // 128, 128),
                residual,
                post_gain[None, :],
                out_weight,
                shared_gate,
                shared_up,
                shared_down,
                gate_weight,
                up_weight,
            ),
        ),
    )
    sent = pl.pallas_call(
        expert_kernel,
        out_shape=pltpu.VMEM((slots, columns), bf16),
        in_specs=[VMEM] * 3 + [HBM] * 3,
        out_specs=VMEM,
        scratch_shapes=[
            pltpu.VMEM((mine - 1, width, inner_width), bf16),
            pltpu.VMEM((mine - 1, width, inner_width), bf16),
            pltpu.VMEM((mine, inner_width, width), bf16),
            pltpu.VMEM((mine, 2 * n_dev, width), bf16),
            pltpu.VMEM((mine, 2 * n_dev, width), bf16),
            pltpu.SemaphoreType.DMA((3 * mine - 2,)),
        ],
        compiler_params=pltpu.CompilerParams(vmem_limit_bytes=24 * MIB),
    )(received, gain, first, in_hbm(gate_weight), in_hbm(up_weight), in_hbm(down_weight))
    returned = exchange(sent)
    return pl.pallas_call(
        combine_kernel,
        out_shape=jax.ShapeDtypeStruct((rows, half), bf16),
        in_specs=[VMEM] * 3,
        out_specs=VMEM,
        compiler_params=pltpu.CompilerParams(vmem_limit_bytes=8 * MIB),
    )(spread, base, returned)


def solution(mesh):
    placed = (
        P("dev", None),
        P("dev", None),
        P("dev", None),
        P("dev", None),
        P("dev"),
        P("dev", None),
        P("dev", None, None),
        P(),
        P(),
        P(),
        P("dev", None),
        P(),
        P("dev", None),
        P("dev", None),
        P("dev", None, None),
        P("dev", None, None),
        P("dev", None, None),
        P(),
        P(),
        P(),
        P(),
    )
    return jax.shard_map(
        on_device, mesh=mesh, in_specs=placed, out_specs=P("dev", "side"), check_vma=False
    )
```

```python
import functools
import jax
import jax.numpy as jnp
from jax import lax
from jax.experimental import pallas as pl
from jax.experimental.pallas import tpu as pltpu
from jax.sharding import PartitionSpec as P

eps = 1e-06
f32 = jnp.float32
bf16 = jnp.bfloat16
i32 = jnp.int32
MIB = 1 << 20


def dot(left, right):
    return jnp.dot(left, right, preferred_element_type=f32)


def iota(shape, axis):
    return lax.broadcasted_iota(i32, shape, axis)


def rms_scale(wide, gain):
    return wide * lax.rsqrt(jnp.mean(wide * wide, axis=-1, keepdims=True) + eps) * gain


def group_order(groups, members, to_groups):
    size = groups * members
    by_group = iota((size, size), 0 if to_groups else 1)
    by_member = iota((size, size), 1 if to_groups else 0)
    wanted = (by_group % members) * groups + by_group // members
    return (wanted == by_member).astype(f32).astype(bf16)


def expert_hits(experts, slot_expert):
    rows, topk = experts.shape
    hits = jnp.zeros((rows, slot_expert.shape[1]), f32)
    for k in range(topk):
        hits = jnp.where(experts[:, k : k + 1] == slot_expert, 1.0, hits)
    earlier = (iota((rows, rows), 1) < iota((rows, rows), 0)).astype(f32).astype(bf16)
    rank = dot(earlier, hits.astype(bf16))
    return hits, rank


def start_all(pairs, sem):
    copies = [
        pltpu.make_async_copy(source, target, sem.at[i]) for i, (source, target) in enumerate(pairs)
    ]
    for copy in copies:
        copy.start()
    return copies


def pieces_of(source, target, count):
    size = source.shape[0] // count
    return [
        (source.at[pl.ds(i * size, size)], target.at[pl.ds(i * size, size)]) for i in range(count)
    ]


def front_kernel(*refs, page, local):
    sources, expert_sources, refs = refs[:12], refs[12:15], refs[15:]
    packed_ref, hidden_ref, attended = refs[:3]
    expert_targets, refs = refs[3:6], refs[6:]
    targets, refs = refs[:12], refs[12:]
    query, prob, valid, chosen, sem, expert_sem = refs
    residual_hbm, pool_hbm, weight_hbm = sources[-3:]
    (
        lengths_ref,
        table_in,
        experts_in,
        queries_ref,
        query_gain_ref,
        keys_ref,
        key_gain_ref,
        values_ref,
        gates_ref,
        residual_ref,
        pool,
        weight,
    ) = targets
    rows, width = queries_ref.shape
    half = width // 2
    head = keys_ref.shape[1]
    heads = width // head
    tokens = pool.shape[0]
    context = 256
    chunks = tokens // context
    weight_parts = 4
    quarter = width // weight_parts
    side = lax.axis_index("side")
    columns_at = pl.ds(pl.multiple_of(side * half, half), half)
    pairs = list(zip(sources, targets))
    copies = start_all(
        pairs[:7]
        + [pairs[10]]
        + pairs[7:9]
        + [
            (residual_hbm.at[:, columns_at], residual_ref),
        ]
        + [
            (source.at[:, columns_at], target)
            for source, target in pieces_of(weight_hbm, weight, weight_parts)
        ],
        sem,
    )
    for copy in copies[:7]:
        copy.wait()

    table = table_in[...].T
    same = iota((rows, rows), 0) == iota((rows, rows), 1)
    lengths = jnp.sum(
        jnp.where(same, jnp.broadcast_to(lengths_ref[...], (rows, rows)), 0), axis=1, keepdims=True
    )
    pages = tokens // page
    number = iota((1, pages), 1)
    limit = jnp.zeros((rows, pages), i32)
    for entry in range(table.shape[1]):
        held = jnp.clip(lengths - entry * page, 0, page)
        limit = jnp.where(table[:, entry : entry + 1] == number, jnp.maximum(limit, held), limit)
    per_chunk = context // page
    limit = limit.astype(f32).astype(bf16)
    limit = jnp.concatenate(
        [limit[:, c * per_chunk : (c + 1) * per_chunk] for c in range(chunks)], axis=0
    )
    expand = iota((per_chunk, context), 1) // page == iota((per_chunk, context), 0)
    limit = dot(limit, expand.astype(f32).astype(bf16))
    valid[...] = (iota((1, context), 1) % page < limit.astype(i32)).astype(f32)

    scale = head ** (-0.5)
    key_normed = rms_scale(keys_ref[...].astype(f32), key_gain_ref[...]).astype(bf16).astype(f32)
    own = []
    for h in range(heads):
        part = queries_ref[:, h * head : (h + 1) * head].astype(f32)
        normed = rms_scale(part, query_gain_ref[...]).astype(bf16)
        query[h * rows : (h + 1) * rows, :] = normed * jnp.asarray(scale, bf16)
        own.append(jnp.sum(normed.astype(f32) * key_normed, axis=-1, keepdims=True))
    own_weight = jnp.exp(jnp.concatenate(own, axis=0) * scale)

    for copy in copies[7:11]:
        copy.wait()
    expert_copies = start_all(
        [
            (source.at[pl.ds(side * (local // 2), local // 2)], target)
            for source, target in zip(expert_sources, expert_targets)
        ],
        expert_sem,
    )
    total = jnp.zeros((heads * rows, context), f32)
    for c in range(chunks):
        at = slice(c * context, (c + 1) * context)
        scores = lax.dot_general(
            query[...],
            pool[at, :head],
            (((1,), (1,)), ((), ())),
            preferred_element_type=f32,
        )
        mask = valid[c * rows : (c + 1) * rows, :]
        weights = (jnp.exp(scores).reshape(heads, rows, context) * mask[None]).reshape(
            heads * rows, context
        )
        total = total + weights
        prob[:, at] = weights.astype(bf16)

    slots, columns = packed_ref.shape
    parts = half // columns
    mine = local // 2
    slot = iota((1, slots), 1)
    per = parts * 2 * mine
    destination = slot // per
    n_dev = slots // per // 2
    expert = (destination % n_dev) * local + (destination // n_dev) * mine + slot % mine
    hits, rank = expert_hits(experts_in[...].T, expert)
    slot_rank = (slot % (2 * mine) // mine).astype(f32)
    picked = jnp.where(rank == slot_rank, hits, 0.0)
    slot_part = slot % per // (2 * mine)
    picked = jnp.concatenate(
        [jnp.where(slot_part == p, picked, 0.0) for p in range(parts)], axis=0
    )
    chosen[...] = picked.T.astype(bf16)

    mixed = dot(prob[...], pool[:, head:])
    inverse = 1.0 / (jnp.sum(total, axis=1, keepdims=True) + own_weight)
    new_values = values_ref[...].astype(f32)
    for h in range(heads):
        part = slice(h * rows, (h + 1) * rows)
        value = (mixed[part] + own_weight[part] * new_values) * inverse[part]
        gate = jax.nn.sigmoid(gates_ref[:, h * head : (h + 1) * head].astype(f32))
        attended[:, h * head : (h + 1) * head] = (value * gate).astype(bf16)

    projected = residual_ref[...].astype(f32)
    for i, copy in enumerate(copies[11:]):
        copy.wait()
        at = slice(i * quarter, (i + 1) * quarter)
        projected = projected + dot(attended[:, at], weight[at, :])
    hidden = projected.astype(bf16)
    hidden_ref[...] = hidden
    stacked = jnp.concatenate(
        [hidden[:, p * columns : (p + 1) * columns] for p in range(parts)], axis=0
    )
    packed_ref[...] = dot(chosen[...], stacked).astype(bf16)
    for copy in expert_copies:
        copy.wait()


def middle_kernel(*refs, n_dev, local):
    (
        attended,
        hidden_ref,
        experts_hbm,
        weights_hbm,
        mix_hbm,
        residual_hbm,
        post_gain_hbm,
        out_weight_hbm,
        shared_gate_hbm,
        shared_up_hbm,
        shared_down_hbm,
        sent_hbm,
    ) = refs[:12]
    base_ref, spread_ref = refs[12:14]
    (
        experts_in,
        weights_in,
        mix,
        residual,
        post_gain,
        out_weight,
        shared_gate,
        shared_up,
        shared_down,
        hidden,
        sem,
    ) = refs[14:]
    rows, width = hidden.shape
    half = width // 2
    mine = local // 2
    side = lax.axis_index("side")
    columns_at = pl.ds(pl.multiple_of(side * half, half), half)
    others_at = pl.ds(pl.multiple_of((1 - side) * half, half), half)
    copies = start_all(
        [
            (experts_hbm, experts_in),
            (weights_hbm, weights_in),
            (mix_hbm, mix),
            (residual_hbm.at[:, others_at], residual),
            (post_gain_hbm, post_gain),
            (out_weight_hbm.at[:, others_at], out_weight),
            (shared_gate_hbm, shared_gate),
            (shared_up_hbm, shared_up),
            (shared_down_hbm.at[:, columns_at], shared_down),
        ],
        sem,
    )
    for copy in copies[:2]:
        copy.wait()
    experts = experts_in[...].T
    weights = weights_in[...].T
    slots = spread_ref.shape[1]
    per = slots // (2 * n_dev)
    parts = per // local
    slot = iota((1, slots), 1)
    source = slot // per
    expert = (source % n_dev) * local + (source // n_dev) * mine + slot % mine
    share = weights / jnp.sum(weights, axis=1, keepdims=True)
    spread = jnp.zeros((rows, slots), f32)
    for k in range(experts.shape[1]):
        spread = jnp.where(experts[:, k : k + 1] == expert, share[:, k : k + 1], spread)
    hits, rank = expert_hits(experts, expert)
    slot_rank = slot % (2 * mine) // mine
    spread = jnp.where(rank == slot_rank.astype(f32), spread, 0.0)
    slot_part = slot % per // (2 * mine)
    for p in range(parts):
        piece = jnp.where(slot_part == p, spread, 0.0)
        high = piece.astype(bf16)
        at = 2 * p * rows
        spread_ref[at : at + rows, :] = high
        spread_ref[at + rows : at + 2 * rows, :] = (piece - high.astype(f32)).astype(bf16)

    for copy in copies[2:]:
        copy.wait()
    mine_hidden = hidden_ref[...]
    hidden[:, columns_at] = mine_hidden
    hidden[:, others_at] = (
        residual[...].astype(f32) + dot(attended[...], out_weight[...])
    ).astype(bf16)
    normed = rms_scale(hidden[...].astype(f32), post_gain[...]).astype(bf16)
    shared_inner = (
        jax.nn.silu(dot(normed, shared_gate[...])) * dot(normed, shared_up[...])
    ).astype(bf16)
    lanes = mix.shape[1]
    logit = jnp.zeros((rows, lanes), f32)
    for i in range(width // lanes):
        logit = logit + normed[:, i * lanes : (i + 1) * lanes].astype(f32) * mix[
            i : i + 1, :
        ].astype(f32)
    scale = jax.nn.sigmoid(jnp.sum(logit, axis=-1, keepdims=True))
    base_ref[...] = mine_hidden.astype(f32) + scale * dot(shared_inner, shared_down[...])


def expert_kernel(received, post_gain, gate, up, down, sent_hbm, taken, result, sent, sem):
    mine, inner_width, width = down.shape
    slots, columns = received.shape
    half = width // 2
    parts = half // columns
    groups = parts * 2 * mine
    n_dev = slots // groups // 2
    block = 32
    inward = group_order(groups, block, True)
    outward = group_order(groups, block, False)

    for s in range(2):
        for b in range(n_dev // block):
            at = (s * n_dev + b * block) * groups
            ordered = dot(inward, received[at : at + groups * block, :]).astype(bf16)
            for p in range(parts):
                for r in range(2):
                    for j in range(mine):
                        at = ((p * 2 + r) * mine + j) * block
                        row = r * n_dev + b * block
                        column = s * half + p * columns
                        taken[j, row : row + block, column : column + columns] = ordered[
                            at : at + block
                        ]
    for j in range(mine):
        normed = rms_scale(taken[j].astype(f32), post_gain[...]).astype(bf16)
        inner = jax.nn.silu(dot(normed, gate[j])) * dot(normed, up[j])
        result[j] = dot(inner.astype(bf16), down[j]).astype(bf16)

    copies = []
    for t in range(2):
        for b in range(n_dev // block):
            gathered = jnp.concatenate(
                [
                    result[
                        j,
                        r * n_dev + b * block : r * n_dev + (b + 1) * block,
                        t * half + p * columns : t * half + (p + 1) * columns,
                    ]
                    for p in range(parts)
                    for r in range(2)
                    for j in range(mine)
                ],
                axis=0,
            )
            at = (t * n_dev + b * block) * groups
            at = pl.ds(at, groups * block)
            sent[at, :] = dot(outward, gathered).astype(bf16)
            copy = pltpu.make_async_copy(sent.at[at], sent_hbm.at[at], sem.at[len(copies)])
            copy.start()
            copies.append(copy)
    for copy in copies:
        copy.wait()


def combine_kernel(spread_ref, base_ref, returned, out_ref):
    rows, half = base_ref.shape
    columns = returned.shape[1]
    routed = dot(spread_ref[...], returned[...])
    for p in range(half // columns):
        at = 2 * p * rows
        value = routed[at : at + rows] + routed[at + rows : at + 2 * rows]
        out_ref[:, p * columns : (p + 1) * columns] = (
            base_ref[:, p * columns : (p + 1) * columns] + value
        ).astype(bf16)


VMEM = pl.BlockSpec(memory_space=pltpu.VMEM)
HBM = pl.BlockSpec(memory_space=pltpu.HBM)


def in_hbm(value):
    return pltpu.with_memory_space_constraint(value, pltpu.HBM)


def exchange(value):
    return lax.all_to_all(value, ("side", "dev"), split_axis=0, concat_axis=0, tiled=True)


def on_device(
    out_gates,
    queries,
    keys_new,
    values_new,
    lengths,
    page_table,
    cache_pool,
    query_gain,
    key_gain,
    out_weight,
    residual,
    post_gain,
    experts,
    route_weights,
    gate_weight,
    up_weight,
    down_weight,
    shared_gate,
    shared_up,
    shared_down,
    shared_mix,
):
    n_dev = lax.axis_size("dev")
    local, width, inner_width = gate_weight.shape
    rows = queries.shape[0]
    head = keys_new.shape[1]
    heads = width // head
    pages, page, both = cache_pool.shape
    tokens = pages * page
    mine = local // 2
    columns = width * mine // 8
    slots = 2 * n_dev * 8
    half = width // 2
    inner_width = gate_weight.shape[2]
    sources = (
        lengths[None, :],
        page_table.T,
        experts.T,
        queries,
        query_gain[None, :],
        keys_new,
        key_gain[None, :],
        values_new,
        out_gates,
        residual,
        cache_pool.reshape(tokens, both),
        out_weight,
    )
    held = [pltpu.VMEM(source.shape, source.dtype) for source in sources]
    held[9] = pltpu.VMEM((rows, half), bf16)
    held[11] = pltpu.VMEM((width, half), bf16)
    packed, hidden, attended, gate, up, down = pl.pallas_call(
        functools.partial(front_kernel, page=page, local=local),
        out_shape=(
            jax.ShapeDtypeStruct((slots, columns), bf16),
            jax.ShapeDtypeStruct((rows, half), bf16),
            jax.ShapeDtypeStruct((rows, width), bf16),
            jax.ShapeDtypeStruct((mine, width, inner_width), bf16),
            jax.ShapeDtypeStruct((mine, width, inner_width), bf16),
            jax.ShapeDtypeStruct((mine, inner_width, width), bf16),
        ),
        in_specs=[HBM] * (len(sources) + 3),
        out_specs=(VMEM,) * 6,
        scratch_shapes=held
        + [
            pltpu.VMEM((heads * rows, head), bf16),
            pltpu.VMEM((heads * rows, tokens), bf16),
            pltpu.VMEM((rows * tokens // 256, 256), f32),
            pltpu.VMEM((slots, half // columns * rows), bf16),
            pltpu.SemaphoreType.DMA((15,)),
            pltpu.SemaphoreType.DMA((3,)),
        ],
        compiler_params=pltpu.CompilerParams(vmem_limit_bytes=24 * MIB),
    )(*map(in_hbm, sources + (gate_weight, up_weight, down_weight)))
    received = exchange(packed)
    sent = pl.pallas_call(
        expert_kernel,
        out_shape=jax.ShapeDtypeStruct((slots, columns), bf16),
        in_specs=[VMEM] * 5,
        out_specs=HBM,
        scratch_shapes=[
            pltpu.VMEM((mine, 2 * n_dev, width), bf16),
            pltpu.VMEM((mine, 2 * n_dev, width), bf16),
            pltpu.VMEM((slots, columns), bf16),
            pltpu.SemaphoreType.DMA((2 * n_dev // 32,)),
        ],
        compiler_params=pltpu.CompilerParams(vmem_limit_bytes=24 * MIB),
    )(received, post_gain[None, :], gate, up, down)
    returned = exchange(sent)
    base, spread = pl.pallas_call(
        functools.partial(middle_kernel, n_dev=n_dev, local=local),
        out_shape=(
            jax.ShapeDtypeStruct((rows, half), f32),
            jax.ShapeDtypeStruct((4 * rows, slots), bf16),
        ),
        in_specs=[VMEM] * 2 + [HBM] * 10,
        out_specs=(VMEM,) * 2,
        scratch_shapes=[
            pltpu.VMEM(experts.T.shape, i32),
            pltpu.VMEM(route_weights.T.shape, f32),
            pltpu.VMEM((width // 128, 128), bf16),
            pltpu.VMEM((rows, half), bf16),
            pltpu.VMEM((1, width), f32),
            pltpu.VMEM((width, half), bf16),
            pltpu.VMEM(shared_gate.shape, bf16),
            pltpu.VMEM(shared_up.shape, bf16),
            pltpu.VMEM((shared_down.shape[0], half), bf16),
            pltpu.VMEM((rows, width), bf16),
            pltpu.SemaphoreType.DMA((9,)),
        ],
        compiler_params=pltpu.CompilerParams(vmem_limit_bytes=24 * MIB),
        cost_estimate=pl.CostEstimate(
            flops=2 * rows * width * (half + 3 * inner_width),
            bytes_accessed=8 * MIB,
            transcendentals=0,
        ),
    )(
        attended,
        hidden,
        *map(
            in_hbm,
            (
                experts.T,
                route_weights.T,
                shared_mix.reshape(width // 128, 128),
                residual,
                post_gain[None, :],
                out_weight,
                shared_gate,
                shared_up,
                shared_down,
                sent,
            ),
        ),
    )
    return pl.pallas_call(
        combine_kernel,
        out_shape=jax.ShapeDtypeStruct((rows, half), bf16),
        in_specs=[VMEM] * 3,
        out_specs=VMEM,
        compiler_params=pltpu.CompilerParams(vmem_limit_bytes=8 * MIB),
    )(spread, base, returned)


def solution(mesh):
    placed = (
        P("dev", None),
        P("dev", None),
        P("dev", None),
        P("dev", None),
        P("dev"),
        P("dev", None),
        P("dev", None, None),
        P(),
        P(),
        P(),
        P("dev", None),
        P(),
        P("dev", None),
        P("dev", None),
        P("dev", None, None),
        P("dev", None, None),
        P("dev", None, None),
        P(),
        P(),
        P(),
        P(),
    )
    return jax.shard_map(
        on_device, mesh=mesh, in_specs=placed, out_specs=P("dev", "side"), check_vma=False
    )
```

```python
import functools
import jax
import jax.numpy as jnp
from jax import lax
from jax.experimental import pallas as pl
from jax.experimental.pallas import tpu as pltpu
from jax.sharding import PartitionSpec as P

eps = 1e-06
f32 = jnp.float32
bf16 = jnp.bfloat16
i32 = jnp.int32
MIB = 1 << 20


def dot(left, right):
    return jnp.dot(left, right, preferred_element_type=f32)


def iota(shape, axis):
    return lax.broadcasted_iota(i32, shape, axis)


def rms_scale(wide, gain):
    return wide * lax.rsqrt(jnp.mean(wide * wide, axis=-1, keepdims=True) + eps) * gain


def group_order(groups, members, to_groups):
    size = groups * members
    by_group = iota((size, size), 0 if to_groups else 1)
    by_member = iota((size, size), 1 if to_groups else 0)
    wanted = (by_group % members) * groups + by_group // members
    return (wanted == by_member).astype(f32).astype(bf16)


def expert_hits(experts, slot_expert):
    rows, topk = experts.shape
    hits = jnp.zeros((rows, slot_expert.shape[1]), f32)
    for k in range(topk):
        hits = jnp.where(experts[:, k : k + 1] == slot_expert, 1.0, hits)
    earlier = (iota((rows, rows), 1) < iota((rows, rows), 0)).astype(f32).astype(bf16)
    rank = dot(earlier, hits.astype(bf16))
    return hits, rank


def start_all(pairs, sem):
    copies = [
        pltpu.make_async_copy(source, target, sem.at[i]) for i, (source, target) in enumerate(pairs)
    ]
    for copy in copies:
        copy.start()
    return copies


def front_kernel(*refs, page, local):
    sources, expert_sources, refs = refs[:12], refs[12:15], refs[15:]
    packed_ref, hidden_ref, attended = refs[:3]
    expert_targets, refs = refs[3:6], refs[6:]
    targets, refs = refs[:12], refs[12:]
    query, prob, valid, own_weight, chosen, sem, expert_sem = refs
    residual_hbm, pool_hbm, weight_hbm = sources[-3:]
    (
        lengths_ref,
        table_in,
        experts_in,
        queries_ref,
        query_gain_ref,
        keys_ref,
        key_gain_ref,
        values_ref,
        gates_ref,
        residual_ref,
        pool,
        weight,
    ) = targets
    rows, width = queries_ref.shape
    half = width // 2
    head = keys_ref.shape[1]
    heads = width // head
    tokens = pool.shape[0]
    context = 256
    chunks = tokens // context
    side = lax.axis_index("side")
    always = side >= 0
    slots, columns = packed_ref.shape
    parts = half // columns
    mine = local // 2
    columns_at = pl.ds(pl.multiple_of(side * half, half), half)
    pairs = list(zip(sources, targets))
    copies = start_all(
        pairs[:7]
        + [pairs[10]]
        + pairs[7:9]
        + [
            (residual_hbm.at[:, columns_at], residual_ref),
            (weight_hbm.at[:, columns_at], weight),
        ],
        sem,
    )
    for copy in copies[:7]:
        copy.wait()

    @pl.when(always)
    def _():
        table = table_in[...].T
        same = iota((rows, rows), 0) == iota((rows, rows), 1)
        lengths = jnp.sum(
            jnp.where(same, jnp.broadcast_to(lengths_ref[...], (rows, rows)), 0), axis=1, keepdims=True
        )
        pages = tokens // page
        number = iota((1, pages), 1)
        limit = jnp.zeros((rows, pages), i32)
        for entry in range(table.shape[1]):
            held = jnp.clip(lengths - entry * page, 0, page)
            limit = jnp.where(table[:, entry : entry + 1] == number, jnp.maximum(limit, held), limit)
        per_chunk = context // page
        limit = limit.astype(f32).astype(bf16)
        limit = jnp.concatenate(
            [limit[:, c * per_chunk : (c + 1) * per_chunk] for c in range(chunks)], axis=0
        )
        expand = iota((per_chunk, context), 1) // page == iota((per_chunk, context), 0)
        limit = dot(limit, expand.astype(f32).astype(bf16))
        valid[...] = (iota((1, context), 1) % page < limit.astype(i32)).astype(f32)

        slot = iota((1, slots), 1)
        per = parts * 2 * mine
        destination = slot // per
        n_dev = slots // per // 2
        expert = (destination % n_dev) * local + (destination // n_dev) * mine + slot % mine
        hits, rank = expert_hits(experts_in[...].T, expert)
        slot_rank = (slot % (2 * mine) // mine).astype(f32)
        picked = jnp.where(rank == slot_rank, hits, 0.0)
        slot_part = slot % per // (2 * mine)
        picked = jnp.concatenate(
            [jnp.where(slot_part == p, picked, 0.0) for p in range(parts)], axis=0
        )
        chosen[...] = picked.T.astype(bf16)

        scale = head ** (-0.5)
        key_normed = rms_scale(keys_ref[...].astype(f32), key_gain_ref[...]).astype(bf16).astype(f32)
        own = []
        for h in range(heads):
            part = queries_ref[:, h * head : (h + 1) * head].astype(f32)
            normed = rms_scale(part, query_gain_ref[...]).astype(bf16)
            query[h * rows : (h + 1) * rows, :] = normed * jnp.asarray(scale, bf16)
            own.append(jnp.sum(normed.astype(f32) * key_normed, axis=-1, keepdims=True))
        own_weight[...] = jnp.exp(jnp.concatenate(own, axis=0) * scale)

    for copy in copies[7:11]:
        copy.wait()
    expert_copies = start_all(
        [
            (source.at[pl.ds(side * mine, target.shape[0])], target)
            for source, target in zip(expert_sources, expert_targets)
        ],
        expert_sem,
    )

    @pl.when(always)
    def _():
        total = jnp.zeros((heads * rows, context), f32)
        for c in range(chunks):
            at = slice(c * context, (c + 1) * context)
            scores = lax.dot_general(
                query[...],
                pool[at, :head],
                (((1,), (1,)), ((), ())),
                preferred_element_type=f32,
            )
            mask = valid[c * rows : (c + 1) * rows, :]
            weights = (jnp.exp(scores).reshape(heads, rows, context) * mask[None]).reshape(
                heads * rows, context
            )
            total = total + weights
            prob[:, at] = weights.astype(bf16)

        middle = heads * rows // 2
        mixed = jnp.concatenate(
            [dot(prob[:middle], pool[:, head:]), dot(prob[middle:], pool[:, head:])], axis=0
        )
        inverse = 1.0 / (jnp.sum(total, axis=1, keepdims=True) + own_weight[...])
        new_values = values_ref[...].astype(f32)
        for h in range(heads):
            part = slice(h * rows, (h + 1) * rows)
            value = (mixed[part] + own_weight[part, :] * new_values) * inverse[part]
            gate = jax.nn.sigmoid(gates_ref[:, h * head : (h + 1) * head].astype(f32))
            attended[:, h * head : (h + 1) * head] = (value * gate).astype(bf16)

    copies[11].wait()

    @pl.when(always)
    def _():
        projected = residual_ref[...].astype(f32) + dot(attended[...], weight[...])
        hidden = projected.astype(bf16)
        hidden_ref[...] = hidden
        stacked = jnp.concatenate(
            [hidden[:, p * columns : (p + 1) * columns] for p in range(parts)], axis=0
        )
        packed_ref[...] = dot(chosen[...], stacked).astype(bf16)

    for copy in expert_copies:
        copy.wait()


def middle_kernel(*refs, n_dev, local):
    (
        attended,
        hidden_ref,
        experts_hbm,
        weights_hbm,
        mix_hbm,
        residual_hbm,
        post_gain_hbm,
        out_weight_hbm,
        shared_gate_hbm,
        shared_up_hbm,
        shared_down_hbm,
        sent_hbm,
    ) = refs[:12]
    base_ref, spread_ref = refs[12:14]
    (
        experts_in,
        weights_in,
        mix,
        residual,
        post_gain,
        out_weight,
        shared_gate,
        shared_up,
        shared_down,
        hidden,
        sem,
    ) = refs[14:]
    rows, width = hidden.shape
    half = width // 2
    mine = local // 2
    side = lax.axis_index("side")
    columns_at = pl.ds(pl.multiple_of(side * half, half), half)
    others_at = pl.ds(pl.multiple_of((1 - side) * half, half), half)
    copies = start_all(
        [
            (experts_hbm, experts_in),
            (weights_hbm, weights_in),
            (mix_hbm, mix),
            (residual_hbm.at[:, others_at], residual),
            (post_gain_hbm, post_gain),
            (out_weight_hbm.at[:, others_at], out_weight),
            (shared_gate_hbm, shared_gate),
            (shared_up_hbm, shared_up),
            (shared_down_hbm.at[:, columns_at], shared_down),
        ],
        sem,
    )
    for copy in copies[:2]:
        copy.wait()
    experts = experts_in[...].T
    weights = weights_in[...].T
    slots = spread_ref.shape[1]
    per = slots // (2 * n_dev)
    parts = per // local
    slot = iota((1, slots), 1)
    source = slot // per
    expert = (source % n_dev) * local + (source // n_dev) * mine + slot % mine
    share = weights / jnp.sum(weights, axis=1, keepdims=True)
    spread = jnp.zeros((rows, slots), f32)
    for k in range(experts.shape[1]):
        spread = jnp.where(experts[:, k : k + 1] == expert, share[:, k : k + 1], spread)
    hits, rank = expert_hits(experts, expert)
    slot_rank = slot % (2 * mine) // mine
    spread = jnp.where(rank == slot_rank.astype(f32), spread, 0.0)
    slot_part = slot % per // (2 * mine)
    for p in range(parts):
        piece = jnp.where(slot_part == p, spread, 0.0)
        high = piece.astype(bf16)
        at = 2 * p * rows
        spread_ref[at : at + rows, :] = high
        spread_ref[at + rows : at + 2 * rows, :] = (piece - high.astype(f32)).astype(bf16)

    for copy in copies[2:]:
        copy.wait()
    mine_hidden = hidden_ref[...]
    hidden[:, columns_at] = mine_hidden
    hidden[:, others_at] = (
        residual[...].astype(f32) + dot(attended[...], out_weight[...])
    ).astype(bf16)
    normed = rms_scale(hidden[...].astype(f32), post_gain[...]).astype(bf16)
    shared_inner = (
        jax.nn.silu(dot(normed, shared_gate[...])) * dot(normed, shared_up[...])
    ).astype(bf16)
    lanes = mix.shape[1]
    logit = jnp.zeros((rows, lanes), f32)
    for i in range(width // lanes):
        logit = logit + normed[:, i * lanes : (i + 1) * lanes].astype(f32) * mix[
            i : i + 1, :
        ].astype(f32)
    scale = jax.nn.sigmoid(jnp.sum(logit, axis=-1, keepdims=True))
    base_ref[...] = mine_hidden.astype(f32) + scale * dot(shared_inner, shared_down[...])


def expert_kernel(
    received,
    post_gain,
    gate,
    up,
    down,
    down_hbm,
    sent_hbm,
    last_down,
    taken,
    inner,
    result,
    sent,
    sem,
):
    mine, width, inner_width = gate.shape
    side = lax.axis_index("side")
    last = pltpu.make_async_copy(
        down_hbm.at[side * mine + mine - 1], last_down, sem.at[sem.shape[0] - 1]
    )
    last.start()
    slots, columns = received.shape
    half = width // 2
    parts = half // columns
    groups = parts * 2 * mine
    n_dev = slots // groups // 2
    block = 32
    inward = group_order(groups, block, True)
    outward = group_order(groups, block, False)

    @pl.when(side >= 0)
    def _():
        for s in range(2):
            for b in range(n_dev // block):
                at = (s * n_dev + b * block) * groups
                ordered = dot(inward, received[at : at + groups * block, :]).astype(bf16)
                for p in range(parts):
                    for r in range(2):
                        for j in range(mine):
                            at = ((p * 2 + r) * mine + j) * block
                            row = r * n_dev + b * block
                            column = s * half + p * columns
                            taken[j, row : row + block, column : column + columns] = ordered[
                                at : at + block
                            ]
        for j in range(mine):
            normed = rms_scale(taken[j].astype(f32), post_gain[...]).astype(bf16)
            inner[j] = (jax.nn.silu(dot(normed, gate[j])) * dot(normed, up[j])).astype(bf16)
        for j in range(mine - 1):
            result[j] = dot(inner[j], down[j]).astype(bf16)

    last.wait()
    result[mine - 1] = dot(inner[mine - 1], last_down[...]).astype(bf16)

    copies = []
    for t in range(2):
        for b in range(n_dev // block):
            gathered = jnp.concatenate(
                [
                    result[
                        j,
                        r * n_dev + b * block : r * n_dev + (b + 1) * block,
                        t * half + p * columns : t * half + (p + 1) * columns,
                    ]
                    for p in range(parts)
                    for r in range(2)
                    for j in range(mine)
                ],
                axis=0,
            )
            at = (t * n_dev + b * block) * groups
            at = pl.ds(at, groups * block)
            sent[at, :] = dot(outward, gathered).astype(bf16)
            copy = pltpu.make_async_copy(sent.at[at], sent_hbm.at[at], sem.at[len(copies)])
            copy.start()
            copies.append(copy)
    for copy in copies:
        copy.wait()


def combine_kernel(spread_ref, base_ref, returned, out_ref):
    rows, half = base_ref.shape
    columns = returned.shape[1]
    routed = dot(spread_ref[...], returned[...])
    for p in range(half // columns):
        at = 2 * p * rows
        value = routed[at : at + rows] + routed[at + rows : at + 2 * rows]
        out_ref[:, p * columns : (p + 1) * columns] = (
            base_ref[:, p * columns : (p + 1) * columns] + value
        ).astype(bf16)


VMEM = pl.BlockSpec(memory_space=pltpu.VMEM)
HBM = pl.BlockSpec(memory_space=pltpu.HBM)


def in_hbm(value):
    return pltpu.with_memory_space_constraint(value, pltpu.HBM)


def exchange(value):
    return lax.all_to_all(value, ("side", "dev"), split_axis=0, concat_axis=0, tiled=True)


def on_device(
    out_gates,
    queries,
    keys_new,
    values_new,
    lengths,
    page_table,
    cache_pool,
    query_gain,
    key_gain,
    out_weight,
    residual,
    post_gain,
    experts,
    route_weights,
    gate_weight,
    up_weight,
    down_weight,
    shared_gate,
    shared_up,
    shared_down,
    shared_mix,
):
    n_dev = lax.axis_size("dev")
    local, width, inner_width = gate_weight.shape
    rows = queries.shape[0]
    head = keys_new.shape[1]
    heads = width // head
    pages, page, both = cache_pool.shape
    tokens = pages * page
    mine = local // 2
    columns = width * mine // 8
    slots = 2 * n_dev * 8
    half = width // 2
    inner_width = gate_weight.shape[2]
    sources = (
        lengths[None, :],
        page_table.T,
        experts.T,
        queries,
        query_gain[None, :],
        keys_new,
        key_gain[None, :],
        values_new,
        out_gates,
        residual,
        cache_pool.reshape(tokens, both),
        out_weight,
    )
    held = [pltpu.VMEM(source.shape, source.dtype) for source in sources]
    held[9] = pltpu.VMEM((rows, half), bf16)
    held[11] = pltpu.VMEM((width, half), bf16)
    packed, hidden, attended, gate, up, down = pl.pallas_call(
        functools.partial(front_kernel, page=page, local=local),
        out_shape=(
            jax.ShapeDtypeStruct((slots, columns), bf16),
            jax.ShapeDtypeStruct((rows, half), bf16),
            jax.ShapeDtypeStruct((rows, width), bf16),
            jax.ShapeDtypeStruct((mine, width, inner_width), bf16),
            jax.ShapeDtypeStruct((mine, width, inner_width), bf16),
            jax.ShapeDtypeStruct((mine - 1, inner_width, width), bf16),
        ),
        in_specs=[HBM] * (len(sources) + 3),
        out_specs=(VMEM,) * 6,
        scratch_shapes=held
        + [
            pltpu.VMEM((heads * rows, head), bf16),
            pltpu.VMEM((heads * rows, tokens), bf16),
            pltpu.VMEM((rows * tokens // 256, 256), f32),
            pltpu.VMEM((heads * rows, 1), f32),
            pltpu.VMEM((slots, half // columns * rows), bf16),
            pltpu.SemaphoreType.DMA((12,)),
            pltpu.SemaphoreType.DMA((3,)),
        ],
        compiler_params=pltpu.CompilerParams(vmem_limit_bytes=24 * MIB),
    )(*map(in_hbm, sources + (gate_weight, up_weight, down_weight)))
    received = exchange(packed)
    sent = pl.pallas_call(
        expert_kernel,
        out_shape=jax.ShapeDtypeStruct((slots, columns), bf16),
        in_specs=[VMEM] * 5 + [HBM],
        out_specs=HBM,
        scratch_shapes=[
            pltpu.VMEM((inner_width, width), bf16),
            pltpu.VMEM((mine, 2 * n_dev, width), bf16),
            pltpu.VMEM((mine, 2 * n_dev, inner_width), bf16),
            pltpu.VMEM((mine, 2 * n_dev, width), bf16),
            pltpu.VMEM((slots, columns), bf16),
            pltpu.SemaphoreType.DMA((2 * n_dev // 32 + 1,)),
        ],
        compiler_params=pltpu.CompilerParams(vmem_limit_bytes=24 * MIB),
    )(received, post_gain[None, :], gate, up, down, in_hbm(down_weight))
    returned = exchange(sent)
    base, spread = pl.pallas_call(
        functools.partial(middle_kernel, n_dev=n_dev, local=local),
        out_shape=(
            jax.ShapeDtypeStruct((rows, half), f32),
            jax.ShapeDtypeStruct((4 * rows, slots), bf16),
        ),
        in_specs=[VMEM] * 2 + [HBM] * 10,
        out_specs=(VMEM,) * 2,
        scratch_shapes=[
            pltpu.VMEM(experts.T.shape, i32),
            pltpu.VMEM(route_weights.T.shape, f32),
            pltpu.VMEM((width // 128, 128), bf16),
            pltpu.VMEM((rows, half), bf16),
            pltpu.VMEM((1, width), f32),
            pltpu.VMEM((width, half), bf16),
            pltpu.VMEM(shared_gate.shape, bf16),
            pltpu.VMEM(shared_up.shape, bf16),
            pltpu.VMEM((shared_down.shape[0], half), bf16),
            pltpu.VMEM((rows, width), bf16),
            pltpu.SemaphoreType.DMA((9,)),
        ],
        compiler_params=pltpu.CompilerParams(vmem_limit_bytes=24 * MIB),
        cost_estimate=pl.CostEstimate(
            flops=2 * rows * width * (half + 3 * inner_width),
            bytes_accessed=8 * MIB,
            transcendentals=0,
        ),
    )(
        attended,
        hidden,
        *map(
            in_hbm,
            (
                experts.T,
                route_weights.T,
                shared_mix.reshape(width // 128, 128),
                residual,
                post_gain[None, :],
                out_weight,
                shared_gate,
                shared_up,
                shared_down,
                sent,
            ),
        ),
    )
    return pl.pallas_call(
        combine_kernel,
        out_shape=jax.ShapeDtypeStruct((rows, half), bf16),
        in_specs=[VMEM] * 3,
        out_specs=VMEM,
        compiler_params=pltpu.CompilerParams(vmem_limit_bytes=8 * MIB),
    )(spread, base, returned)


def solution(mesh):
    placed = (
        P("dev", None),
        P("dev", None),
        P("dev", None),
        P("dev", None),
        P("dev"),
        P("dev", None),
        P("dev", None, None),
        P(),
        P(),
        P(),
        P("dev", None),
        P(),
        P("dev", None),
        P("dev", None),
        P("dev", None, None),
        P("dev", None, None),
        P("dev", None, None),
        P(),
        P(),
        P(),
        P(),
    )
    return jax.shard_map(
        on_device, mesh=mesh, in_specs=placed, out_specs=P("dev", "side"), check_vma=False
    )
```

```python
import functools
import jax
import jax.numpy as jnp
from jax import lax
from jax.experimental import pallas as pl
from jax.experimental.pallas import tpu as pltpu
from jax.sharding import PartitionSpec as P

eps = 1e-06
f32 = jnp.float32
bf16 = jnp.bfloat16
i32 = jnp.int32
MIB = 1 << 20


def dot(left, right):
    return jnp.dot(left, right, preferred_element_type=f32)


def iota(shape, axis):
    return lax.broadcasted_iota(i32, shape, axis)


def rms_scale(wide, gain):
    return wide * lax.rsqrt(jnp.mean(wide * wide, axis=-1, keepdims=True) + eps) * gain


def group_order(groups, members, to_groups):
    size = groups * members
    by_group = iota((size, size), 0 if to_groups else 1)
    by_member = iota((size, size), 1 if to_groups else 0)
    wanted = (by_group % members) * groups + by_group // members
    return (wanted == by_member).astype(f32).astype(bf16)


def expert_hits(experts, slot_expert):
    rows, topk = experts.shape
    hits = jnp.zeros((rows, slot_expert.shape[1]), f32)
    for k in range(topk):
        hits = jnp.where(experts[:, k : k + 1] == slot_expert, 1.0, hits)
    earlier = (iota((rows, rows), 1) < iota((rows, rows), 0)).astype(f32).astype(bf16)
    rank = dot(earlier, hits.astype(bf16))
    return hits, rank


def start_all(pairs, sem):
    copies = [
        pltpu.make_async_copy(source, target, sem.at[i]) for i, (source, target) in enumerate(pairs)
    ]
    for copy in copies:
        copy.start()
    return copies


def front_kernel(*refs, page, local):
    sources, refs = refs[:12], refs[12:]
    packed_ref, hidden_ref, attended = refs[:3]
    refs = refs[3:]
    targets, refs = refs[:12], refs[12:]
    query, prob, valid, own_weight, chosen, sem = refs
    residual_hbm, pool_hbm, weight_hbm = sources[-3:]
    (
        lengths_ref,
        table_in,
        experts_in,
        queries_ref,
        query_gain_ref,
        keys_ref,
        key_gain_ref,
        values_ref,
        gates_ref,
        residual_ref,
        pool,
        weight,
    ) = targets
    rows, width = queries_ref.shape
    half = width // 2
    head = keys_ref.shape[1]
    heads = width // head
    tokens = pool.shape[0]
    context = 256
    chunks = tokens // context
    side = lax.axis_index("side")
    always = side >= 0
    slots, columns = packed_ref.shape
    parts = half // columns
    mine = local // 2
    columns_at = pl.ds(pl.multiple_of(side * half, half), half)
    pairs = list(zip(sources, targets))
    copies = start_all(
        pairs[:7]
        + [pairs[10]]
        + pairs[7:9]
        + [
            (residual_hbm.at[:, columns_at], residual_ref),
            (weight_hbm.at[:, columns_at], weight),
        ],
        sem,
    )
    for copy in copies[:7]:
        copy.wait()

    @pl.when(always)
    def _():
        table = table_in[...].T
        same = iota((rows, rows), 0) == iota((rows, rows), 1)
        lengths = jnp.sum(
            jnp.where(same, jnp.broadcast_to(lengths_ref[...], (rows, rows)), 0), axis=1, keepdims=True
        )
        pages = tokens // page
        number = iota((1, pages), 1)
        limit = jnp.zeros((rows, pages), i32)
        for entry in range(table.shape[1]):
            held = jnp.clip(lengths - entry * page, 0, page)
            limit = jnp.where(table[:, entry : entry + 1] == number, jnp.maximum(limit, held), limit)
        per_chunk = context // page
        limit = limit.astype(f32).astype(bf16)
        limit = jnp.concatenate(
            [limit[:, c * per_chunk : (c + 1) * per_chunk] for c in range(chunks)], axis=0
        )
        expand = iota((per_chunk, context), 1) // page == iota((per_chunk, context), 0)
        limit = dot(limit, expand.astype(f32).astype(bf16))
        valid[...] = (iota((1, context), 1) % page < limit.astype(i32)).astype(f32)

        slot = iota((1, slots), 1)
        per = parts * 2 * mine
        destination = slot // per
        n_dev = slots // per // 2
        expert = (destination % n_dev) * local + (destination // n_dev) * mine + slot % mine
        hits, rank = expert_hits(experts_in[...].T, expert)
        slot_rank = (slot % (2 * mine) // mine).astype(f32)
        picked = jnp.where(rank == slot_rank, hits, 0.0)
        slot_part = slot % per // (2 * mine)
        picked = jnp.concatenate(
            [jnp.where(slot_part == p, picked, 0.0) for p in range(parts)], axis=0
        )
        chosen[...] = picked.T.astype(bf16)

        scale = head ** (-0.5)
        key_normed = rms_scale(keys_ref[...].astype(f32), key_gain_ref[...]).astype(bf16).astype(f32)
        own = []
        for h in range(heads):
            part = queries_ref[:, h * head : (h + 1) * head].astype(f32)
            normed = rms_scale(part, query_gain_ref[...]).astype(bf16)
            query[h * rows : (h + 1) * rows, :] = normed * jnp.asarray(scale, bf16)
            own.append(jnp.sum(normed.astype(f32) * key_normed, axis=-1, keepdims=True))
        own_weight[...] = jnp.exp(jnp.concatenate(own, axis=0) * scale)

    for copy in copies[7:11]:
        copy.wait()

    @pl.when(always)
    def _():
        total = jnp.zeros((heads * rows, context), f32)
        for c in range(chunks):
            at = slice(c * context, (c + 1) * context)
            scores = lax.dot_general(
                query[...],
                pool[at, :head],
                (((1,), (1,)), ((), ())),
                preferred_element_type=f32,
            )
            mask = valid[c * rows : (c + 1) * rows, :]
            weights = (jnp.exp(scores).reshape(heads, rows, context) * mask[None]).reshape(
                heads * rows, context
            )
            total = total + weights
            prob[:, at] = weights.astype(bf16)

        middle = heads * rows // 2
        mixed = jnp.concatenate(
            [dot(prob[:middle], pool[:, head:]), dot(prob[middle:], pool[:, head:])], axis=0
        )
        inverse = 1.0 / (jnp.sum(total, axis=1, keepdims=True) + own_weight[...])
        new_values = values_ref[...].astype(f32)
        for h in range(heads):
            part = slice(h * rows, (h + 1) * rows)
            value = (mixed[part] + own_weight[part, :] * new_values) * inverse[part]
            gate = jax.nn.sigmoid(gates_ref[:, h * head : (h + 1) * head].astype(f32))
            attended[:, h * head : (h + 1) * head] = (value * gate).astype(bf16)

    copies[-1].wait()

    @pl.when(always)
    def _():
        projected = residual_ref[...].astype(f32) + dot(attended[...], weight[...])
        hidden = projected.astype(bf16)
        hidden_ref[...] = hidden
        stacked = jnp.concatenate(
            [hidden[:, p * columns : (p + 1) * columns] for p in range(parts)], axis=0
        )
        packed_ref[...] = dot(chosen[...], stacked).astype(bf16)


def middle_kernel(*refs, n_dev, local):
    (
        attended,
        hidden_ref,
        experts_hbm,
        weights_hbm,
        mix_hbm,
        residual_hbm,
        post_gain_hbm,
        out_weight_hbm,
        shared_gate_hbm,
        shared_up_hbm,
        shared_down_hbm,
        sent_hbm,
    ) = refs[:12]
    base_ref, spread_ref = refs[12:14]
    (
        experts_in,
        weights_in,
        mix,
        residual,
        post_gain,
        out_weight,
        shared_gate,
        shared_up,
        shared_down,
        hidden,
        sem,
    ) = refs[14:]
    rows, width = hidden.shape
    half = width // 2
    mine = local // 2
    side = lax.axis_index("side")
    columns_at = pl.ds(pl.multiple_of(side * half, half), half)
    others_at = pl.ds(pl.multiple_of((1 - side) * half, half), half)
    copies = start_all(
        [
            (experts_hbm, experts_in),
            (weights_hbm, weights_in),
            (mix_hbm, mix),
            (residual_hbm.at[:, others_at], residual),
            (post_gain_hbm, post_gain),
            (out_weight_hbm.at[:, others_at], out_weight),
            (shared_gate_hbm, shared_gate),
            (shared_up_hbm, shared_up),
            (shared_down_hbm.at[:, columns_at], shared_down),
        ],
        sem,
    )
    for copy in copies[:2]:
        copy.wait()
    experts = experts_in[...].T
    weights = weights_in[...].T
    slots = spread_ref.shape[1]
    per = slots // (2 * n_dev)
    parts = per // local
    slot = iota((1, slots), 1)
    source = slot // per
    expert = (source % n_dev) * local + (source // n_dev) * mine + slot % mine
    share = weights / jnp.sum(weights, axis=1, keepdims=True)
    spread = jnp.zeros((rows, slots), f32)
    for k in range(experts.shape[1]):
        spread = jnp.where(experts[:, k : k + 1] == expert, share[:, k : k + 1], spread)
    hits, rank = expert_hits(experts, expert)
    slot_rank = slot % (2 * mine) // mine
    spread = jnp.where(rank == slot_rank.astype(f32), spread, 0.0)
    slot_part = slot % per // (2 * mine)
    for p in range(parts):
        piece = jnp.where(slot_part == p, spread, 0.0)
        high = piece.astype(bf16)
        at = 2 * p * rows
        spread_ref[at : at + rows, :] = high
        spread_ref[at + rows : at + 2 * rows, :] = (piece - high.astype(f32)).astype(bf16)

    for copy in copies[2:]:
        copy.wait()
    mine_hidden = hidden_ref[...]
    hidden[:, columns_at] = mine_hidden
    hidden[:, others_at] = (
        residual[...].astype(f32) + dot(attended[...], out_weight[...])
    ).astype(bf16)
    normed = rms_scale(hidden[...].astype(f32), post_gain[...]).astype(bf16)
    shared_inner = (
        jax.nn.silu(dot(normed, shared_gate[...])) * dot(normed, shared_up[...])
    ).astype(bf16)
    lanes = mix.shape[1]
    logit = jnp.zeros((rows, lanes), f32)
    for i in range(width // lanes):
        logit = logit + normed[:, i * lanes : (i + 1) * lanes].astype(f32) * mix[
            i : i + 1, :
        ].astype(f32)
    scale = jax.nn.sigmoid(jnp.sum(logit, axis=-1, keepdims=True))
    base_ref[...] = mine_hidden.astype(f32) + scale * dot(shared_inner, shared_down[...])


def expert_kernel(
    received,
    post_gain,
    gate,
    up,
    down,
    sent_hbm,
    taken,
    result,
    sent,
    sem,
):
    local, width, inner_width = gate.shape
    mine = local // 2
    first = lax.axis_index("side") * mine
    slots, columns = received.shape
    half = width // 2
    parts = half // columns
    groups = parts * 2 * mine
    n_dev = slots // groups // 2
    block = 32
    inward = group_order(groups, block, True)
    outward = group_order(groups, block, False)

    for s in range(2):
        for b in range(n_dev // block):
            at = (s * n_dev + b * block) * groups
            ordered = dot(inward, received[at : at + groups * block, :]).astype(bf16)
            for p in range(parts):
                for r in range(2):
                    for j in range(mine):
                        at = ((p * 2 + r) * mine + j) * block
                        row = r * n_dev + b * block
                        column = s * half + p * columns
                        taken[j, row : row + block, column : column + columns] = ordered[
                            at : at + block
                        ]
    for j in range(mine):
        normed = rms_scale(taken[j].astype(f32), post_gain[...]).astype(bf16)
        inner = jax.nn.silu(dot(normed, gate[first + j])) * dot(normed, up[first + j])
        result[j] = dot(inner.astype(bf16), down[first + j]).astype(bf16)

    copies = []
    for t in range(2):
        for b in range(n_dev // block):
            gathered = jnp.concatenate(
                [
                    result[
                        j,
                        r * n_dev + b * block : r * n_dev + (b + 1) * block,
                        t * half + p * columns : t * half + (p + 1) * columns,
                    ]
                    for p in range(parts)
                    for r in range(2)
                    for j in range(mine)
                ],
                axis=0,
            )
            at = (t * n_dev + b * block) * groups
            at = pl.ds(at, groups * block)
            sent[at, :] = dot(outward, gathered).astype(bf16)
            copy = pltpu.make_async_copy(sent.at[at], sent_hbm.at[at], sem.at[len(copies)])
            copy.start()
            copies.append(copy)
    for copy in copies:
        copy.wait()


def combine_kernel(spread_ref, base_ref, returned, out_ref):
    rows, half = base_ref.shape
    columns = returned.shape[1]
    routed = dot(spread_ref[...], returned[...])
    for p in range(half // columns):
        at = 2 * p * rows
        value = routed[at : at + rows] + routed[at + rows : at + 2 * rows]
        out_ref[:, p * columns : (p + 1) * columns] = (
            base_ref[:, p * columns : (p + 1) * columns] + value
        ).astype(bf16)


VMEM = pl.BlockSpec(memory_space=pltpu.VMEM)
HBM = pl.BlockSpec(memory_space=pltpu.HBM)


def in_hbm(value):
    return pltpu.with_memory_space_constraint(value, pltpu.HBM)


def in_vmem(value):
    return pltpu.with_memory_space_constraint(value, pltpu.VMEM)


def exchange(value):
    return lax.all_to_all(value, ("side", "dev"), split_axis=0, concat_axis=0, tiled=True)


def on_device(
    out_gates,
    queries,
    keys_new,
    values_new,
    lengths,
    page_table,
    cache_pool,
    query_gain,
    key_gain,
    out_weight,
    residual,
    post_gain,
    experts,
    route_weights,
    gate_weight,
    up_weight,
    down_weight,
    shared_gate,
    shared_up,
    shared_down,
    shared_mix,
):
    n_dev = lax.axis_size("dev")
    local, width, inner_width = gate_weight.shape
    rows = queries.shape[0]
    head = keys_new.shape[1]
    heads = width // head
    pages, page, both = cache_pool.shape
    tokens = pages * page
    mine = local // 2
    columns = width * mine // 8
    slots = 2 * n_dev * 8
    half = width // 2
    inner_width = gate_weight.shape[2]
    sources = (
        lengths[None, :],
        page_table.T,
        experts.T,
        queries,
        query_gain[None, :],
        keys_new,
        key_gain[None, :],
        values_new,
        out_gates,
        residual,
        cache_pool.reshape(tokens, both),
        out_weight,
    )
    held = [pltpu.VMEM(source.shape, source.dtype) for source in sources]
    held[9] = pltpu.VMEM((rows, half), bf16)
    held[11] = pltpu.VMEM((width, half), bf16)
    packed, hidden, attended = pl.pallas_call(
        functools.partial(front_kernel, page=page, local=local),
        out_shape=(
            jax.ShapeDtypeStruct((slots, columns), bf16),
            jax.ShapeDtypeStruct((rows, half), bf16),
            jax.ShapeDtypeStruct((rows, width), bf16),
        ),
        in_specs=[HBM] * len(sources),
        out_specs=(VMEM,) * 3,
        scratch_shapes=held
        + [
            pltpu.VMEM((heads * rows, head), bf16),
            pltpu.VMEM((heads * rows, tokens), bf16),
            pltpu.VMEM((rows * tokens // 256, 256), f32),
            pltpu.VMEM((heads * rows, 1), f32),
            pltpu.VMEM((slots, half // columns * rows), bf16),
            pltpu.SemaphoreType.DMA((12,)),
        ],
        compiler_params=pltpu.CompilerParams(vmem_limit_bytes=24 * MIB),
    )(*map(in_hbm, sources))
    received = exchange(packed)
    sent = pl.pallas_call(
        expert_kernel,
        out_shape=jax.ShapeDtypeStruct((slots, columns), bf16),
        in_specs=[VMEM] * 5,
        out_specs=HBM,
        scratch_shapes=[
            pltpu.VMEM((mine, 2 * n_dev, width), bf16),
            pltpu.VMEM((mine, 2 * n_dev, width), bf16),
            pltpu.VMEM((slots, columns), bf16),
            pltpu.SemaphoreType.DMA((2 * n_dev // 32,)),
        ],
        compiler_params=pltpu.CompilerParams(vmem_limit_bytes=24 * MIB),
    )(received, post_gain[None, :], *map(in_vmem, (gate_weight, up_weight, down_weight)))
    returned = exchange(sent)
    base, spread = pl.pallas_call(
        functools.partial(middle_kernel, n_dev=n_dev, local=local),
        out_shape=(
            jax.ShapeDtypeStruct((rows, half), f32),
            jax.ShapeDtypeStruct((4 * rows, slots), bf16),
        ),
        in_specs=[VMEM] * 2 + [HBM] * 10,
        out_specs=(VMEM,) * 2,
        scratch_shapes=[
            pltpu.VMEM(experts.T.shape, i32),
            pltpu.VMEM(route_weights.T.shape, f32),
            pltpu.VMEM((width // 128, 128), bf16),
            pltpu.VMEM((rows, half), bf16),
            pltpu.VMEM((1, width), f32),
            pltpu.VMEM((width, half), bf16),
            pltpu.VMEM(shared_gate.shape, bf16),
            pltpu.VMEM(shared_up.shape, bf16),
            pltpu.VMEM((shared_down.shape[0], half), bf16),
            pltpu.VMEM((rows, width), bf16),
            pltpu.SemaphoreType.DMA((9,)),
        ],
        compiler_params=pltpu.CompilerParams(vmem_limit_bytes=24 * MIB),
        cost_estimate=pl.CostEstimate(
            flops=2 * rows * width * (half + 3 * inner_width),
            bytes_accessed=8 * MIB,
            transcendentals=0,
        ),
    )(
        attended,
        hidden,
        *map(
            in_hbm,
            (
                experts.T,
                route_weights.T,
                shared_mix.reshape(width // 128, 128),
                residual,
                post_gain[None, :],
                out_weight,
                shared_gate,
                shared_up,
                shared_down,
                sent,
            ),
        ),
    )
    return pl.pallas_call(
        combine_kernel,
        out_shape=jax.ShapeDtypeStruct((rows, half), bf16),
        in_specs=[VMEM] * 3,
        out_specs=VMEM,
        compiler_params=pltpu.CompilerParams(vmem_limit_bytes=8 * MIB),
    )(spread, base, returned)


def solution(mesh):
    placed = (
        P("dev", None),
        P("dev", None),
        P("dev", None),
        P("dev", None),
        P("dev"),
        P("dev", None),
        P("dev", None, None),
        P(),
        P(),
        P(),
        P("dev", None),
        P(),
        P("dev", None),
        P("dev", None),
        P("dev", None, None),
        P("dev", None, None),
        P("dev", None, None),
        P(),
        P(),
        P(),
        P(),
    )
    return jax.shard_map(
        on_device, mesh=mesh, in_specs=placed, out_specs=P("dev", "side"), check_vma=False
    )
```

```python
import functools
import jax
import jax.numpy as jnp
from jax import lax
from jax.experimental import pallas as pl
from jax.experimental.pallas import tpu as pltpu
from jax.sharding import PartitionSpec as P

eps = 1e-06
f32 = jnp.float32
bf16 = jnp.bfloat16
i32 = jnp.int32
MIB = 1 << 20


def dot(left, right):
    return jnp.dot(left, right, preferred_element_type=f32)


def iota(shape, axis):
    return lax.broadcasted_iota(i32, shape, axis)


def rms_scale(wide, gain):
    return wide * lax.rsqrt(jnp.mean(wide * wide, axis=-1, keepdims=True) + eps) * gain


def group_order(groups, members, to_groups):
    size = groups * members
    by_group = iota((size, size), 0 if to_groups else 1)
    by_member = iota((size, size), 1 if to_groups else 0)
    wanted = (by_group % members) * groups + by_group // members
    return (wanted == by_member).astype(f32).astype(bf16)


def expert_hits(experts, slot_expert):
    rows, topk = experts.shape
    hits = jnp.zeros((rows, slot_expert.shape[1]), f32)
    for k in range(topk):
        hits = jnp.where(experts[:, k : k + 1] == slot_expert, 1.0, hits)
    earlier = (iota((rows, rows), 1) < iota((rows, rows), 0)).astype(f32).astype(bf16)
    rank = dot(earlier, hits.astype(bf16))
    return hits, rank


def start_all(pairs, sem):
    copies = [
        pltpu.make_async_copy(source, target, sem.at[i]) for i, (source, target) in enumerate(pairs)
    ]
    for copy in copies:
        copy.start()
    return copies


def front_kernel(*refs, page, local):
    sources, refs = refs[:12], refs[12:]
    packed_ref, hidden_ref, attended = refs[:3]
    refs = refs[3:]
    targets, refs = refs[:12], refs[12:]
    query, prob, valid, own_weight, chosen, total, sem = refs
    residual_hbm, pool_hbm, weight_hbm = sources[-3:]
    (
        lengths_ref,
        table_in,
        experts_in,
        queries_ref,
        query_gain_ref,
        keys_ref,
        key_gain_ref,
        values_ref,
        gates_ref,
        residual_ref,
        pool,
        weight,
    ) = targets
    rows, width = queries_ref.shape
    half = width // 2
    head = keys_ref.shape[1]
    heads = width // head
    tokens = pool.shape[0]
    context = 256
    chunks = tokens // context
    side = lax.axis_index("side")
    always = side >= 0
    slots, columns = packed_ref.shape
    parts = half // columns
    mine = local // 2
    columns_at = pl.ds(pl.multiple_of(side * half, half), half)
    pairs = list(zip(sources, targets))
    copies = start_all(
        pairs[:7]
        + [
            (pool_hbm.at[:, pl.ds(i * head, head)], pool.at[:, pl.ds(i * head, head)])
            for i in range(2)
        ]
        + pairs[7:9]
        + [
            (residual_hbm.at[:, columns_at], residual_ref),
            (weight_hbm.at[:, columns_at], weight),
        ],
        sem,
    )
    for copy in copies[:7]:
        copy.wait()

    @pl.when(always)
    def _():
        table = table_in[...].T
        same = iota((rows, rows), 0) == iota((rows, rows), 1)
        lengths = jnp.sum(
            jnp.where(same, jnp.broadcast_to(lengths_ref[...], (rows, rows)), 0), axis=1, keepdims=True
        )
        pages = tokens // page
        number = iota((1, pages), 1)
        limit = jnp.zeros((rows, pages), i32)
        for entry in range(table.shape[1]):
            held = jnp.clip(lengths - entry * page, 0, page)
            limit = jnp.where(table[:, entry : entry + 1] == number, jnp.maximum(limit, held), limit)
        per_chunk = context // page
        limit = limit.astype(f32).astype(bf16)
        limit = jnp.concatenate(
            [limit[:, c * per_chunk : (c + 1) * per_chunk] for c in range(chunks)], axis=0
        )
        expand = iota((per_chunk, context), 1) // page == iota((per_chunk, context), 0)
        limit = dot(limit, expand.astype(f32).astype(bf16))
        valid[...] = (iota((1, context), 1) % page < limit.astype(i32)).astype(f32)

        slot = iota((1, slots), 1)
        per = parts * 2 * mine
        destination = slot // per
        n_dev = slots // per // 2
        expert = (destination % n_dev) * local + (destination // n_dev) * mine + slot % mine
        hits, rank = expert_hits(experts_in[...].T, expert)
        slot_rank = (slot % (2 * mine) // mine).astype(f32)
        picked = jnp.where(rank == slot_rank, hits, 0.0)
        slot_part = slot % per // (2 * mine)
        picked = jnp.concatenate(
            [jnp.where(slot_part == p, picked, 0.0) for p in range(parts)], axis=0
        )
        chosen[...] = picked.T.astype(bf16)

        scale = head ** (-0.5)
        key_normed = rms_scale(keys_ref[...].astype(f32), key_gain_ref[...]).astype(bf16).astype(f32)
        own = []
        for h in range(heads):
            part = queries_ref[:, h * head : (h + 1) * head].astype(f32)
            normed = rms_scale(part, query_gain_ref[...]).astype(bf16)
            query[h * rows : (h + 1) * rows, :] = normed * jnp.asarray(scale, bf16)
            own.append(jnp.sum(normed.astype(f32) * key_normed, axis=-1, keepdims=True))
        own_weight[...] = jnp.exp(jnp.concatenate(own, axis=0) * scale)

    copies[7].wait()

    @pl.when(always)
    def _():
        summed = jnp.zeros((heads * rows, context), f32)
        for c in range(chunks):
            at = slice(c * context, (c + 1) * context)
            scores = lax.dot_general(
                query[...],
                pool[at, :head],
                (((1,), (1,)), ((), ())),
                preferred_element_type=f32,
            )
            mask = valid[c * rows : (c + 1) * rows, :]
            weights = (jnp.exp(scores).reshape(heads, rows, context) * mask[None]).reshape(
                heads * rows, context
            )
            summed = summed + weights
            prob[:, at] = weights.astype(bf16)
        total[...] = summed

    for copy in copies[8:12]:
        copy.wait()

    @pl.when(always)
    def _():
        middle = heads * rows // 2
        mixed = jnp.concatenate(
            [dot(prob[:middle], pool[:, head:]), dot(prob[middle:], pool[:, head:])], axis=0
        )
        inverse = 1.0 / (jnp.sum(total[...], axis=1, keepdims=True) + own_weight[...])
        new_values = values_ref[...].astype(f32)
        for h in range(heads):
            part = slice(h * rows, (h + 1) * rows)
            value = (mixed[part] + own_weight[part, :] * new_values) * inverse[part]
            gate = jax.nn.sigmoid(gates_ref[:, h * head : (h + 1) * head].astype(f32))
            attended[:, h * head : (h + 1) * head] = (value * gate).astype(bf16)

    copies[-1].wait()

    @pl.when(always)
    def _():
        projected = residual_ref[...].astype(f32) + dot(attended[...], weight[...])
        hidden = projected.astype(bf16)
        hidden_ref[...] = hidden
        stacked = jnp.concatenate(
            [hidden[:, p * columns : (p + 1) * columns] for p in range(parts)], axis=0
        )
        packed_ref[...] = dot(chosen[...], stacked).astype(bf16)


def middle_kernel(*refs, n_dev, local):
    (
        attended,
        hidden_ref,
        experts_hbm,
        weights_hbm,
        mix_hbm,
        residual_hbm,
        post_gain_hbm,
        out_weight_hbm,
        shared_gate_hbm,
        shared_up_hbm,
        shared_down_hbm,
        sent_hbm,
    ) = refs[:12]
    base_ref, spread_ref = refs[12:14]
    (
        experts_in,
        weights_in,
        mix,
        residual,
        post_gain,
        out_weight,
        shared_gate,
        shared_up,
        shared_down,
        hidden,
        sem,
    ) = refs[14:]
    rows, width = hidden.shape
    half = width // 2
    mine = local // 2
    side = lax.axis_index("side")
    columns_at = pl.ds(pl.multiple_of(side * half, half), half)
    others_at = pl.ds(pl.multiple_of((1 - side) * half, half), half)
    copies = start_all(
        [
            (experts_hbm, experts_in),
            (weights_hbm, weights_in),
            (mix_hbm, mix),
            (residual_hbm.at[:, others_at], residual),
            (post_gain_hbm, post_gain),
            (out_weight_hbm.at[:, others_at], out_weight),
            (shared_gate_hbm, shared_gate),
            (shared_up_hbm, shared_up),
            (shared_down_hbm.at[:, columns_at], shared_down),
        ],
        sem,
    )
    for copy in copies[:2]:
        copy.wait()
    experts = experts_in[...].T
    weights = weights_in[...].T
    slots = spread_ref.shape[1]
    per = slots // (2 * n_dev)
    parts = per // local
    slot = iota((1, slots), 1)
    source = slot // per
    expert = (source % n_dev) * local + (source // n_dev) * mine + slot % mine
    share = weights / jnp.sum(weights, axis=1, keepdims=True)
    spread = jnp.zeros((rows, slots), f32)
    for k in range(experts.shape[1]):
        spread = jnp.where(experts[:, k : k + 1] == expert, share[:, k : k + 1], spread)
    hits, rank = expert_hits(experts, expert)
    slot_rank = slot % (2 * mine) // mine
    spread = jnp.where(rank == slot_rank.astype(f32), spread, 0.0)
    slot_part = slot % per // (2 * mine)
    for p in range(parts):
        piece = jnp.where(slot_part == p, spread, 0.0)
        high = piece.astype(bf16)
        at = 2 * p * rows
        spread_ref[at : at + rows, :] = high
        spread_ref[at + rows : at + 2 * rows, :] = (piece - high.astype(f32)).astype(bf16)

    for copy in copies[2:]:
        copy.wait()
    mine_hidden = hidden_ref[...]
    hidden[:, columns_at] = mine_hidden
    hidden[:, others_at] = (
        residual[...].astype(f32) + dot(attended[...], out_weight[...])
    ).astype(bf16)
    normed = rms_scale(hidden[...].astype(f32), post_gain[...]).astype(bf16)
    shared_inner = (
        jax.nn.silu(dot(normed, shared_gate[...])) * dot(normed, shared_up[...])
    ).astype(bf16)
    lanes = mix.shape[1]
    logit = jnp.zeros((rows, lanes), f32)
    for i in range(width // lanes):
        logit = logit + normed[:, i * lanes : (i + 1) * lanes].astype(f32) * mix[
            i : i + 1, :
        ].astype(f32)
    scale = jax.nn.sigmoid(jnp.sum(logit, axis=-1, keepdims=True))
    base_ref[...] = mine_hidden.astype(f32) + scale * dot(shared_inner, shared_down[...])


def expert_kernel(
    received,
    post_gain,
    gate,
    up,
    down,
    sent_hbm,
    taken,
    result,
    sent,
    sem,
):
    local, width, inner_width = gate.shape
    mine = local // 2
    first = lax.axis_index("side") * mine
    slots, columns = received.shape
    half = width // 2
    parts = half // columns
    groups = parts * 2 * mine
    n_dev = slots // groups // 2
    block = 32
    inward = group_order(groups, block, True)
    outward = group_order(groups, block, False)

    for s in range(2):
        for b in range(n_dev // block):
            at = (s * n_dev + b * block) * groups
            ordered = dot(inward, received[at : at + groups * block, :]).astype(bf16)
            for p in range(parts):
                for r in range(2):
                    for j in range(mine):
                        at = ((p * 2 + r) * mine + j) * block
                        row = r * n_dev + b * block
                        column = s * half + p * columns
                        taken[j, row : row + block, column : column + columns] = ordered[
                            at : at + block
                        ]
    for j in range(mine):
        normed = rms_scale(taken[j].astype(f32), post_gain[...]).astype(bf16)
        inner = jax.nn.silu(dot(normed, gate[first + j])) * dot(normed, up[first + j])
        result[j] = dot(inner.astype(bf16), down[first + j]).astype(bf16)

    copies = []
    for t in range(2):
        for b in range(n_dev // block):
            gathered = jnp.concatenate(
                [
                    result[
                        j,
                        r * n_dev + b * block : r * n_dev + (b + 1) * block,
                        t * half + p * columns : t * half + (p + 1) * columns,
                    ]
                    for p in range(parts)
                    for r in range(2)
                    for j in range(mine)
                ],
                axis=0,
            )
            at = (t * n_dev + b * block) * groups
            at = pl.ds(at, groups * block)
            sent[at, :] = dot(outward, gathered).astype(bf16)
            copy = pltpu.make_async_copy(sent.at[at], sent_hbm.at[at], sem.at[len(copies)])
            copy.start()
            copies.append(copy)
    for copy in copies:
        copy.wait()


def combine_kernel(spread_ref, base_ref, returned, out_ref):
    rows, half = base_ref.shape
    columns = returned.shape[1]
    routed = dot(spread_ref[...], returned[...])
    for p in range(half // columns):
        at = 2 * p * rows
        value = routed[at : at + rows] + routed[at + rows : at + 2 * rows]
        out_ref[:, p * columns : (p + 1) * columns] = (
            base_ref[:, p * columns : (p + 1) * columns] + value
        ).astype(bf16)


VMEM = pl.BlockSpec(memory_space=pltpu.VMEM)
HBM = pl.BlockSpec(memory_space=pltpu.HBM)


def in_hbm(value):
    return pltpu.with_memory_space_constraint(value, pltpu.HBM)


def in_vmem(value):
    return pltpu.with_memory_space_constraint(value, pltpu.VMEM)


def exchange(value):
    return lax.all_to_all(value, ("side", "dev"), split_axis=0, concat_axis=0, tiled=True)


def on_device(
    out_gates,
    queries,
    keys_new,
    values_new,
    lengths,
    page_table,
    cache_pool,
    query_gain,
    key_gain,
    out_weight,
    residual,
    post_gain,
    experts,
    route_weights,
    gate_weight,
    up_weight,
    down_weight,
    shared_gate,
    shared_up,
    shared_down,
    shared_mix,
):
    n_dev = lax.axis_size("dev")
    local, width, inner_width = gate_weight.shape
    rows = queries.shape[0]
    head = keys_new.shape[1]
    heads = width // head
    pages, page, both = cache_pool.shape
    tokens = pages * page
    mine = local // 2
    columns = width * mine // 8
    slots = 2 * n_dev * 8
    half = width // 2
    inner_width = gate_weight.shape[2]
    sources = (
        lengths[None, :],
        page_table.T,
        experts.T,
        queries,
        query_gain[None, :],
        keys_new,
        key_gain[None, :],
        values_new,
        out_gates,
        residual,
        cache_pool.reshape(tokens, both),
        out_weight,
    )
    held = [pltpu.VMEM(source.shape, source.dtype) for source in sources]
    held[9] = pltpu.VMEM((rows, half), bf16)
    held[11] = pltpu.VMEM((width, half), bf16)
    packed, hidden, attended = pl.pallas_call(
        functools.partial(front_kernel, page=page, local=local),
        out_shape=(
            jax.ShapeDtypeStruct((slots, columns), bf16),
            jax.ShapeDtypeStruct((rows, half), bf16),
            jax.ShapeDtypeStruct((rows, width), bf16),
        ),
        in_specs=[HBM] * len(sources),
        out_specs=(VMEM,) * 3,
        scratch_shapes=held
        + [
            pltpu.VMEM((heads * rows, head), bf16),
            pltpu.VMEM((heads * rows, tokens), bf16),
            pltpu.VMEM((rows * tokens // 256, 256), f32),
            pltpu.VMEM((heads * rows, 1), f32),
            pltpu.VMEM((slots, half // columns * rows), bf16),
            pltpu.VMEM((heads * rows, 256), f32),
            pltpu.SemaphoreType.DMA((13,)),
        ],
        compiler_params=pltpu.CompilerParams(vmem_limit_bytes=24 * MIB),
    )(*map(in_hbm, sources))
    received = exchange(packed)
    sent = pl.pallas_call(
        expert_kernel,
        out_shape=jax.ShapeDtypeStruct((slots, columns), bf16),
        in_specs=[VMEM] * 5,
        out_specs=HBM,
        scratch_shapes=[
            pltpu.VMEM((mine, 2 * n_dev, width), bf16),
            pltpu.VMEM((mine, 2 * n_dev, width), bf16),
            pltpu.VMEM((slots, columns), bf16),
            pltpu.SemaphoreType.DMA((2 * n_dev // 32,)),
        ],
        compiler_params=pltpu.CompilerParams(vmem_limit_bytes=24 * MIB),
    )(received, post_gain[None, :], *map(in_vmem, (gate_weight, up_weight, down_weight)))
    returned = exchange(sent)
    base, spread = pl.pallas_call(
        functools.partial(middle_kernel, n_dev=n_dev, local=local),
        out_shape=(
            jax.ShapeDtypeStruct((rows, half), f32),
            jax.ShapeDtypeStruct((4 * rows, slots), bf16),
        ),
        in_specs=[VMEM] * 2 + [HBM] * 10,
        out_specs=(VMEM,) * 2,
        scratch_shapes=[
            pltpu.VMEM(experts.T.shape, i32),
            pltpu.VMEM(route_weights.T.shape, f32),
            pltpu.VMEM((width // 128, 128), bf16),
            pltpu.VMEM((rows, half), bf16),
            pltpu.VMEM((1, width), f32),
            pltpu.VMEM((width, half), bf16),
            pltpu.VMEM(shared_gate.shape, bf16),
            pltpu.VMEM(shared_up.shape, bf16),
            pltpu.VMEM((shared_down.shape[0], half), bf16),
            pltpu.VMEM((rows, width), bf16),
            pltpu.SemaphoreType.DMA((9,)),
        ],
        compiler_params=pltpu.CompilerParams(vmem_limit_bytes=24 * MIB),
        cost_estimate=pl.CostEstimate(
            flops=2 * rows * width * (half + 3 * inner_width),
            bytes_accessed=8 * MIB,
            transcendentals=0,
        ),
    )(
        attended,
        hidden,
        *map(
            in_hbm,
            (
                experts.T,
                route_weights.T,
                shared_mix.reshape(width // 128, 128),
                residual,
                post_gain[None, :],
                out_weight,
                shared_gate,
                shared_up,
                shared_down,
                sent,
            ),
        ),
    )
    return pl.pallas_call(
        combine_kernel,
        out_shape=jax.ShapeDtypeStruct((rows, half), bf16),
        in_specs=[VMEM] * 3,
        out_specs=VMEM,
        compiler_params=pltpu.CompilerParams(vmem_limit_bytes=8 * MIB),
    )(spread, base, returned)


def solution(mesh):
    placed = (
        P("dev", None),
        P("dev", None),
        P("dev", None),
        P("dev", None),
        P("dev"),
        P("dev", None),
        P("dev", None, None),
        P(),
        P(),
        P(),
        P("dev", None),
        P(),
        P("dev", None),
        P("dev", None),
        P("dev", None, None),
        P("dev", None, None),
        P("dev", None, None),
        P(),
        P(),
        P(),
        P(),
    )
    return jax.shard_map(
        on_device, mesh=mesh, in_specs=placed, out_specs=P("dev", "side"), check_vma=False
    )
```
